128 devices in a mesh: gx: 4 (over z), gy: 32 (over y, x, core).
Axes of the slice: x: 4, y: 4, z: 4, core: 2. Of those that a mesh axis runs over, the one named last changes fastest.
Arguments:
- embeddings: bfloat16 [1572864, 256], P(('gx', 'gy'))
- start: float32 [32, 1572864], P(None, ('gx', 'gy'))
- requests: int32 [128, 32], P(('gx', 'gy')), may hold values from -1 to 23, as said below
- pairs: int32 [128, 64, 2], P(('gx', 'gy')), may hold values from 0 to 55, as said below
- counts: int32 [128], P(('gx', 'gy')), may hold values from 24 to 64, as said below
Outputs:
- spectral: float32 [32, 1572864], P(None, ('gx', 'gy'))
The draws below stay inside these ranges and needn't reach their ends.
Inputs may be any that keep to these rules, and one draw needn't show every extreme that they name: requests[d, q] is -1 where q is d's own index along gy; every entry that is not -1 is used by some live slot of d. A live slot (a, s) has a < 24; if s < 24 then a <= s, else requests[d, s - 24] >= 0; every block of a device has a live slot (a, a); local pairs of one device are distinct; slots at or beyond counts[d] are (0, 0). counts[d] = 24 + (entries of requests[d] that are not -1) + (slots pairing two different blocks of d); in every gx group some device has all 64 slots live.
All inputs are finite; a program needn't handle non-finite values.
Results may differ from the reference program's by a relative error of at most 0.0046.
Values may be sent and summed in bfloat16 or wider, within the bound.
No kernel may reach another device: no remote copies, remote signals or barrier semaphores. Data moves between devices by JAX's collectives and lax.ppermute only.
A program may use at most 192 MiB of HBM per device.

```python
import math
import jax
import jax.numpy as jnp
from jax import lax

D = 256
VECS = 32
BLK = 512
BLOCKS_DEV = 24
EXTRA = 9
ITERS = 2
ROW_DEV = 12288
ROWS = 1572864
SLOTS = 64
N_GX = 4
N_GY = 32


def device_slots(key, wanted, extra_count):
    peer_count = wanted.shape[0]
    key_row, key_local, key_order = jax.random.split(key, 3)
    diag_ids = jnp.arange(BLOCKS_DEV, dtype=jnp.int32)
    remote_rows = jax.random.randint(key_row, (peer_count,), 0, BLOCKS_DEV, dtype=jnp.int32)
    remote_cols = BLOCKS_DEV + jnp.arange(peer_count, dtype=jnp.int32)
    candidate = jax.random.permutation(key_local, BLOCKS_DEV * BLOCKS_DEV).astype(jnp.int32)
    cand_row = candidate // BLOCKS_DEV
    cand_col = candidate % BLOCKS_DEV
    upper_first = jnp.argsort(jnp.where(cand_row < cand_col, 0, 1), stable=True)[:EXTRA]
    local_rows = cand_row[upper_first]
    local_cols = cand_col[upper_first]
    all_rows = jnp.concatenate([diag_ids, remote_rows, local_rows])
    all_cols = jnp.concatenate([diag_ids, remote_cols, local_cols])
    alive = jnp.concatenate([jnp.ones((BLOCKS_DEV,), bool), wanted, jnp.arange(EXTRA) < extra_count])
    entry_total = all_rows.shape[0]
    shuffle = jax.random.permutation(key_order, entry_total).astype(jnp.int32)
    order_key = jnp.where(alive, 0, entry_total) + shuffle
    slot_order = jnp.argsort(order_key)
    slot_total = entry_total - 1
    picked_live = alive[slot_order][:slot_total]
    rows_out = jnp.where(picked_live, all_rows[slot_order][:slot_total], 0)
    cols_out = jnp.where(picked_live, all_cols[slot_order][:slot_total], 0)
    return jnp.stack([rows_out, cols_out], axis=-1).astype(jnp.int32)


def plan(key):
    peer_count = SLOTS - BLOCKS_DEV - EXTRA + 1
    device_total = ROWS // ROW_DEV
    group_total = device_total // peer_count
    key_busy, key_want, key_pick, key_extra, key_slot = jax.random.split(key, 5)
    device = jnp.arange(device_total, dtype=jnp.int32)
    minor_index = device % peer_count
    major_index = device // peer_count
    crowded = minor_index == jax.random.randint(key_busy, (group_total,), 0, peer_count, dtype=jnp.int32)[major_index]
    peer_ids = jnp.arange(peer_count, dtype=jnp.int32)
    wanted = (jax.random.randint(key_want, (device_total, peer_count), 0, 2, dtype=jnp.int32) == 1) | crowded[:, None]
    wanted = wanted & (peer_ids[None, :] != minor_index[:, None])
    requests = jnp.where(wanted, jax.random.randint(key_pick, (device_total, peer_count), 0, BLOCKS_DEV, dtype=jnp.int32), -1)
    extra_count = jnp.where(crowded, EXTRA, jax.random.randint(key_extra, (device_total,), 0, EXTRA + 1, dtype=jnp.int32))
    counts = (BLOCKS_DEV + jnp.sum(wanted.astype(jnp.int32), axis=1) + extra_count).astype(jnp.int32)
    pairs = jax.vmap(device_slots)(jax.random.split(key_slot, device_total), wanted, extra_count)
    return (requests.astype(jnp.int32), pairs, counts)


def draw_requests(key, part):
    shared = plan(key)
    return shared[0]


def draw_pairs(key, part):
    shared = plan(key)
    return shared[1]


def draw_counts(key, part):
    shared = plan(key)
    return shared[2]


def draw_embeddings(key, part):
    key = jax.random.fold_in(key, 22)
    key_centre, key_voice, key_jitter, key_scale = jax.random.split(key, 4)
    voices = max(2, BLK // 32)
    centres = jax.random.normal(key_centre, (voices, D), jnp.float32)
    voice_ids = jax.random.randint(key_voice, (ROWS,), 0, voices, dtype=jnp.int32)
    jitter = jax.random.normal(key_jitter, (ROWS, D), jnp.float32)
    row_scale = jnp.exp(jax.random.uniform(key_scale, (ROWS, 1), jnp.float32, math.log(0.5), math.log(8.0)))
    return ((0.6 * centres[voice_ids] + 0.8 * jitter) * row_scale).astype(jnp.bfloat16)


def draw_start(key, part):
    key = jax.random.fold_in(key, 21)
    key_column, key_row, key_basis = jax.random.split(key, 3)
    column = jnp.exp(jax.random.uniform(key_column, (VECS, 1), jnp.float32, 0.0, math.log(10.0)))
    row_factor = jnp.exp(jax.random.uniform(key_row, (1, ROWS), jnp.float32, 0.0, math.log(10.0)))
    rising = jnp.exp(math.log(3.0) * jnp.arange(ROWS, dtype=jnp.float32) / ROWS)[None, :]
    basis = jax.random.normal(key_basis, (VECS, ROWS), jnp.float32)
    return (basis * column * row_factor * rising).astype(jnp.float32)


def setup_inputs(seed: int = 0) -> dict:
    splits = jax.random.split(jax.random.key(seed), 6)
    embeddings = draw_embeddings(jax.random.fold_in(splits[5], 71), 0)
    start = draw_start(jax.random.fold_in(splits[5], 71), 0)
    requests = draw_requests(jax.random.fold_in(splits[5], 71), 0)
    pairs = draw_pairs(jax.random.fold_in(splits[5], 71), 0)
    counts = draw_counts(jax.random.fold_in(splits[5], 71), 0)
    return {"embeddings": embeddings, "start": start, "requests": requests, "pairs": pairs, "counts": counts}


def normalize(raw_rows):
    values = raw_rows.astype(jnp.float32)
    scaled = values * lax.rsqrt(lax.optimization_barrier(jnp.sum(values * values, axis=-1, keepdims=True)) + 1e-06)
    return scaled.astype(jnp.bfloat16)

def make_tiles(left_rows, right_rows):
    product = jnp.einsum('srd,scd->src', left_rows.astype(jnp.float32), right_rows.astype(jnp.float32), precision=lax.Precision.HIGHEST)
    return (product * product * product).astype(jnp.bfloat16)

def apply_tiles(units, rounded, row_block, col_block, live_weight, twice):
    block_total = units.shape[0]
    vec_blocks = rounded.reshape(VECS, block_total, BLK).transpose(1, 0, 2)

    def device_pass(total, slot_data):
        rows_index, cols_index, live_row, live_col = slot_data
        tile_stack = make_tiles(units[rows_index], units[cols_index]).astype(jnp.float32)
        row_vecs = vec_blocks[rows_index].astype(jnp.float32)
        col_vecs = vec_blocks[cols_index].astype(jnp.float32)
        to_row = jnp.einsum('skc,src->skr', col_vecs, tile_stack, precision=lax.Precision.HIGHEST) * live_row[:, None, None]
        to_col = jnp.einsum('skr,src->skc', row_vecs, tile_stack, precision=lax.Precision.HIGHEST) * live_col[:, None, None]
        total = total.at[rows_index].add(to_row).at[cols_index].add(to_col)
        return (total, None)
    empty = jnp.zeros((block_total, VECS, BLK), jnp.float32)
    total = lax.scan(device_pass, empty, (row_block, col_block, live_weight, twice))[0]
    return total.transpose(1, 0, 2).reshape(VECS, block_total * BLK)

def orthonormalize(image):
    gram_matrix = jnp.dot(image.astype(jnp.float32), image.T.astype(jnp.float32), precision=lax.Precision.HIGHEST, preferred_element_type=jnp.float32)
    lower_factor = jnp.linalg.cholesky(gram_matrix / ROWS)
    return lax.linalg.triangular_solve(lower_factor, image, left_side=True, lower=True)

def reference(embeddings, start, requests, pairs, counts):
    device_total = N_GX * N_GY
    block_total = device_total * BLOCKS_DEV
    units = lax.map(normalize, embeddings.reshape(device_total, ROW_DEV, D)).reshape(block_total, BLK, D)
    device = jnp.arange(device_total, dtype=jnp.int32)[:, None]
    row_local = pairs[:, :, 0].astype(jnp.int32)
    col_local = pairs[:, :, 1].astype(jnp.int32)
    peer_slot = jnp.clip(col_local - BLOCKS_DEV, 0, N_GY - 1).astype(jnp.int32)
    peer_block = jnp.maximum(jnp.take_along_axis(requests, peer_slot, axis=1), 0).astype(jnp.int32)
    remote_block = (device // N_GY * N_GY + peer_slot) * BLOCKS_DEV + peer_block
    row_block = (device * BLOCKS_DEV + row_local).astype(jnp.int32)
    col_block = jnp.where(col_local < BLOCKS_DEV, device * BLOCKS_DEV + col_local, remote_block).astype(jnp.int32)
    slot_live = jnp.arange(SLOTS, dtype=jnp.int32)[None, :] < counts[:, None]
    live_weight = slot_live.astype(jnp.float32)
    twice = (slot_live & (row_block != col_block)).astype(jnp.float32)
    vectors = start
    for iteration in range(ITERS):
        image = apply_tiles(units, vectors.astype(jnp.bfloat16), row_block, col_block, live_weight, twice)
        vectors = orthonormalize(image)
    return vectors
```

```python
import functools

import jax
import jax.numpy as jnp
from jax import lax
from jax.experimental import pallas as pl
from jax.experimental.pallas import tpu as pltpu
from jax.sharding import PartitionSpec as P

D = 256
VECS = 32
BLK = 512
ITERS = 2
HALF = BLK // 2
EXTRA = 9

FAR_ROW = 0
LOCAL = 32
LOCAL_COUNT = 96
TABLE = 128

NT = (((1,), (1,)), ((), ()))
NN = (((1,), (0,)), ((), ()))
SMEM = pl.BlockSpec(memory_space=pltpu.SMEM)
VMEM = pl.BlockSpec(memory_space=pltpu.VMEM)
ANY = pl.BlockSpec(memory_space=pl.ANY)
LOOKAHEAD = 3
BUFFERS = 4


def columns_of(block):
    return pl.ds(pl.multiple_of(block * BLK, BLK), BLK)


def params(limit_mib=48):
    return pltpu.CompilerParams(vmem_limit_bytes=limit_mib * 1024 * 1024)


def cost(flops, bytes_accessed):
    return pl.CostEstimate(flops=flops, bytes_accessed=bytes_accessed, transcendentals=0)


def prepare_kernel(pairs, counts, raw, unit, send, table, held, head, following, sem):
    block = pl.program_id(0)
    block_count = held.shape[0]
    peer_count = send.shape[0]

    @pl.when(block == 0)
    def _():
        def clear(i, _):
            table[i] = -1
            return 0

        lax.fori_loop(0, TABLE, clear, 0)

        def clear_head(i, _):
            head[i] = -1
            return 0

        lax.fori_loop(0, block_count, clear_head, 0)

        def note(k, local_count):
            row = pairs[k, 0]
            col = pairs[k, 1]
            far = col >= block_count

            @pl.when(far)
            def _():
                peer = col - block_count
                table[FAR_ROW + peer] = row
                following[peer] = head[row]
                head[row] = peer

            @pl.when(jnp.logical_not(far))
            def _():
                table[LOCAL + local_count] = row * 64 + col

            return local_count + jnp.where(far, 0, 1)

        table[LOCAL_COUNT] = lax.fori_loop(0, counts[0], note, 0)

    values = raw[...].astype(jnp.float32)
    scaled = values * lax.rsqrt(jnp.sum(values * values, axis=-1, keepdims=True) + 1e-06)
    rounded = scaled.astype(jnp.bfloat16)
    unit[0] = rounded
    held[block] = rounded

    def copy(peer, row):
        return pltpu.make_async_copy(held.at[row], send.at[peer], sem.at[peer])

    def emit(peer):
        copy(peer, block).start()
        return following[peer]

    lax.while_loop(lambda peer: peer >= 0, emit, head[block])

    @pl.when(block == block_count - 1)
    def _():
        def finish(peer, _):
            row = table[FAR_ROW + peer]

            @pl.when(row >= 0)
            def _():
                copy(peer, row).wait()

            return 0

        lax.fori_loop(0, peer_count, finish, 0)


def prepare(embeddings, pairs, counts, peer_count):
    block_count = embeddings.shape[0] // BLK
    return pl.pallas_call(
        prepare_kernel,
        grid=(block_count,),
        in_specs=[SMEM, SMEM, pl.BlockSpec((BLK, D), lambda b: (b, 0))],
        out_specs=[pl.BlockSpec((1, BLK, D), lambda b: (b, 0, 0)), ANY, SMEM],
        out_shape=[
            jax.ShapeDtypeStruct((block_count, BLK, D), jnp.bfloat16),
            jax.ShapeDtypeStruct((peer_count, BLK, D), jnp.bfloat16),
            jax.ShapeDtypeStruct((TABLE,), jnp.int32),
        ],
        scratch_shapes=[
            pltpu.VMEM((block_count, BLK, D), jnp.bfloat16),
            pltpu.SMEM((block_count,), jnp.int32),
            pltpu.SMEM((peer_count,), jnp.int32),
            pltpu.SemaphoreType.DMA((peer_count,)),
        ],
        compiler_params=params(),
        cost_estimate=cost(10**7, 20 * 2**20),
        name="prepare",
    )(pairs, counts, embeddings)


def spread(table, source, out):
    def one(peer, _):
        row = table[FAR_ROW + peer]

        @pl.when(row >= 0)
        def _():
            out[peer] = source[:, columns_of(row)]

        @pl.when(row < 0)
        def _():
            out[peer] = jnp.zeros(out.shape[1:], out.dtype)

        return 0

    lax.fori_loop(0, out.shape[0], one, 0)


def first_vectors_kernel(table, start, rounded, out):
    rounded[...] = start[...].astype(jnp.bfloat16)
    spread(table, rounded, out)


def first_vectors(table, start, peer_count):
    return pl.pallas_call(
        first_vectors_kernel,
        in_specs=[SMEM, VMEM],
        out_specs=[VMEM, VMEM],
        out_shape=[
            jax.ShapeDtypeStruct(start.shape, jnp.bfloat16),
            jax.ShapeDtypeStruct((peer_count, VECS, BLK), jnp.bfloat16),
        ],
        compiler_params=params(),
        cost_estimate=cost(10**6, 4 * 2**20),
        name="first_vectors",
    )(table, start)


def half_tile(left, right):
    product = lax.dot_general(left, right, NT, preferred_element_type=jnp.float32)
    return (product * product * product).astype(jnp.bfloat16)


def dot_nt(vecs, tile):
    return lax.dot_general(vecs, tile, NT, preferred_element_type=jnp.float32)


def dot_nn(vecs, tile):
    return lax.dot_general(vecs, tile, NN, preferred_element_type=jnp.float32)


def apply_local(rounded, total, row, col, tile):
    total[:, columns_of(row)] += dot_nt(rounded[:, columns_of(col)], tile[...])

    @pl.when(row != col)
    def _():
        total[:, columns_of(col)] += dot_nn(rounded[:, columns_of(row)], tile[...])


def local_build_kernel(table, units, rounded, total, tiles, buffer, sem):
    count = table[LOCAL_COUNT]
    total[...] = jnp.zeros_like(total)

    def copy(n):
        return pltpu.make_async_copy(buffer.at[n % 2], tiles.at[n], sem.at[n % 2])

    def one(n, _):
        code = table[LOCAL + n]
        row = code // 64
        col = code % 64

        @pl.when(n >= 2)
        def _():
            copy(n - 2).wait()

        tile = buffer.at[n % 2]
        for h in range(2):
            rows = pl.ds(h * HALF, HALF)
            tile[rows, :] = half_tile(units[row, rows, :], units[col])
        copy(n).start()
        apply_local(rounded, total, row, col, tile)
        return 0

    lax.fori_loop(0, count, one, 0)

    @pl.when(count >= 2)
    def _():
        copy(count - 2).wait()

    @pl.when(count >= 1)
    def _():
        copy(count - 1).wait()


def local_build(table, units, rounded):
    block_count = units.shape[0]
    return pl.pallas_call(
        local_build_kernel,
        in_specs=[SMEM, VMEM, VMEM],
        out_specs=[VMEM, ANY],
        out_shape=[
            jax.ShapeDtypeStruct(rounded.shape, jnp.float32),
            jax.ShapeDtypeStruct((block_count + EXTRA, BLK, BLK), jnp.bfloat16),
        ],
        scratch_shapes=[
            pltpu.VMEM((2, BLK, BLK), jnp.bfloat16),
            pltpu.SemaphoreType.DMA((2,)),
        ],
        compiler_params=params(),
        cost_estimate=cost(33 * 2 * BLK * BLK * (D + 8 * VECS), 26 * 2**20),
        name="local_build",
    )(table, units, rounded)


def note_active(wanted, active):
    def one(peer, count):
        @pl.when(wanted[peer] >= 0)
        def _():
            active[count] = peer

        return count + jnp.where(wanted[peer] >= 0, 1, 0)

    return lax.fori_loop(0, wanted.shape[0], one, 0)


def far_build_kernel(wanted, units, far_rows, rounded, back, tiles, active, near, far, buffer, load_sem, save_sem):
    count = note_active(wanted, active)

    def loads(n):
        peer = active[n]
        return (
            pltpu.make_async_copy(far_rows.at[peer], far.at[n], load_sem.at[0, n]),
            pltpu.make_async_copy(units.at[wanted[peer]], near.at[n], load_sem.at[1, n]),
        )

    def begin(n):
        @pl.when(n < count)
        def _():
            for load in loads(n):
                load.start()

    def copy(n):
        return pltpu.make_async_copy(buffer.at[n % 2], tiles.at[active[n]], save_sem.at[n % 2])

    for n in range(LOOKAHEAD):
        begin(n)

    def one(n, _):
        peer = active[n]
        begin(n + LOOKAHEAD)

        @pl.when(n >= 2)
        def _():
            copy(n - 2).wait()

        for load in loads(n):
            load.wait()
        vecs = rounded[:, columns_of(wanted[peer])]
        tile = buffer.at[n % 2]
        for h in range(2):
            rows = pl.ds(h * HALF, HALF)
            part = half_tile(far[n, rows, :], near[n])
            tile[rows, :] = part
            back[peer, :, rows] = dot_nt(vecs, part).astype(jnp.bfloat16)
        copy(n).start()
        return 0

    lax.fori_loop(0, count, one, 0)

    @pl.when(count >= 2)
    def _():
        copy(count - 2).wait()

    @pl.when(count >= 1)
    def _():
        copy(count - 1).wait()


def far_build(wanted, units, far_rows, rounded):
    peer_count = far_rows.shape[0]
    return pl.pallas_call(
        far_build_kernel,
        in_specs=[SMEM, ANY, ANY, VMEM],
        out_specs=[VMEM, ANY],
        out_shape=[
            jax.ShapeDtypeStruct((peer_count, VECS, BLK), jnp.bfloat16),
            jax.ShapeDtypeStruct((peer_count, BLK, BLK), jnp.bfloat16),
        ],
        scratch_shapes=[
            pltpu.SMEM((peer_count,), jnp.int32),
            pltpu.VMEM((peer_count, BLK, D), jnp.bfloat16),
            pltpu.VMEM((peer_count, BLK, D), jnp.bfloat16),
            pltpu.VMEM((2, BLK, BLK), jnp.bfloat16),
            pltpu.SemaphoreType.DMA((2, peer_count)),
            pltpu.SemaphoreType.DMA((2,)),
        ],
        compiler_params=params(),
        cost_estimate=cost(32 * 2 * BLK * BLK * (D + 4 * VECS), 34 * 2**20),
        name="far_build",
    )(wanted, units, far_rows, rounded)


def stream(count, source_of, buffer, sem, use):
    def load(n):
        return pltpu.make_async_copy(source_of(n), buffer.at[n % BUFFERS], sem.at[n % BUFFERS])

    def begin(n):
        @pl.when(n < count)
        def _():
            load(n).start()

    for n in range(BUFFERS - 1):
        begin(n)

    def one(n, _):
        begin(n + BUFFERS - 1)
        load(n).wait()
        use(n, buffer.at[n % BUFFERS])
        return 0

    lax.fori_loop(0, count, one, 0)


def tile_scratch():
    return [
        pltpu.VMEM((BUFFERS, BLK, BLK), jnp.bfloat16),
        pltpu.SemaphoreType.DMA((BUFFERS,)),
    ]


def far_back_kernel(wanted, tiles, rounded, back, active, buffer, sem):
    count = note_active(wanted, active)

    def use(n, tile):
        peer = active[n]
        vecs = rounded[:, columns_of(wanted[peer])]
        back[peer] = dot_nt(vecs, tile[...]).astype(jnp.bfloat16)

    stream(count, lambda n: tiles.at[active[n]], buffer, sem, use)


def far_back(wanted, tiles, rounded):
    peer_count = tiles.shape[0]
    return pl.pallas_call(
        far_back_kernel,
        in_specs=[SMEM, ANY, VMEM],
        out_specs=VMEM,
        out_shape=jax.ShapeDtypeStruct((peer_count, VECS, BLK), jnp.bfloat16),
        scratch_shapes=[pltpu.SMEM((peer_count,), jnp.int32), *tile_scratch()],
        compiler_params=params(),
        cost_estimate=cost(32 * 2 * BLK * BLK * 4 * VECS, 17 * 2**20),
        name="far_back",
    )(wanted, tiles, rounded)


def far_own_kernel(wanted, tiles, far_vecs, before, total, active, buffer, sem):
    count = note_active(wanted, active)
    total[...] = before[...]

    def use(n, tile):
        peer = active[n]
        total[:, columns_of(wanted[peer])] += dot_nn(far_vecs[peer], tile[...])

    stream(count, lambda n: tiles.at[active[n]], buffer, sem, use)


def far_own(wanted, tiles, far_vecs, before):
    peer_count = tiles.shape[0]
    return pl.pallas_call(
        far_own_kernel,
        in_specs=[SMEM, ANY, VMEM, VMEM],
        out_specs=VMEM,
        out_shape=jax.ShapeDtypeStruct(before.shape, jnp.float32),
        scratch_shapes=[pltpu.SMEM((peer_count,), jnp.int32), *tile_scratch()],
        compiler_params=params(),
        cost_estimate=cost(32 * 2 * BLK * BLK * 4 * VECS, 20 * 2**20),
        name="far_own",
    )(wanted, tiles, far_vecs, before)


def local_apply_kernel(table, tiles, rounded, total, buffer, sem):
    total[...] = jnp.zeros_like(total)

    def use(n, tile):
        code = table[LOCAL + n]
        apply_local(rounded, total, code // 64, code % 64, tile)

    stream(table[LOCAL_COUNT], lambda n: tiles.at[n], buffer, sem, use)


def local_apply(table, tiles, rounded):
    return pl.pallas_call(
        local_apply_kernel,
        in_specs=[SMEM, ANY, VMEM],
        out_specs=VMEM,
        out_shape=jax.ShapeDtypeStruct(rounded.shape, jnp.float32),
        scratch_shapes=tile_scratch(),
        compiler_params=params(),
        cost_estimate=cost(33 * 2 * BLK * BLK * 8 * VECS, 18 * 2**20),
        name="local_apply",
    )(table, tiles, rounded)


def assemble_kernel(table, own, returned, image, gram):
    image[...] = own[...]

    def one(peer, _):
        row = table[FAR_ROW + peer]

        @pl.when(row >= 0)
        def _():
            image[:, columns_of(row)] += returned[peer].astype(jnp.float32)

        return 0

    lax.fori_loop(0, returned.shape[0], one, 0)

    def product(block, total):
        part = image[:, columns_of(block)]
        return total + lax.dot_general(
            part, part, NT, precision=lax.Precision.HIGHEST, preferred_element_type=jnp.float32
        )

    gram[...] = lax.fori_loop(0, image.shape[1] // BLK, product, jnp.zeros((VECS, VECS), jnp.float32))


def assemble(table, own, returned):
    return pl.pallas_call(
        assemble_kernel,
        in_specs=[SMEM, VMEM, VMEM],
        out_specs=[VMEM, VMEM],
        out_shape=[
            jax.ShapeDtypeStruct(own.shape, jnp.float32),
            jax.ShapeDtypeStruct((VECS, VECS), jnp.float32),
        ],
        compiler_params=params(),
        cost_estimate=cost(10**8, 5 * 2**20),
        name="assemble",
    )(table, own, returned)


def inverse_factor(matrix):
    rows = lax.broadcasted_iota(jnp.int32, (VECS, VECS), 0)
    lanes = lax.broadcasted_iota(jnp.int32, (VECS, VECS), 1)
    inverse = jnp.where(rows == lanes, 1.0, 0.0).astype(jnp.float32)
    for k in range(VECS):
        scale = lax.rsqrt(matrix[k : k + 1, k : k + 1])
        pivot_row = matrix[k : k + 1, :] * scale
        inverse_row = inverse[k : k + 1, :] * scale
        factor = jnp.where(rows > k, matrix[:, k : k + 1] * scale, 0.0)
        matrix = matrix - factor * pivot_row
        inverse = jnp.where(rows == k, inverse_row, inverse - factor * inverse_row)
    return inverse


def solve_into(inverse, image, block):
    return lax.dot_general(
        inverse,
        image[:, columns_of(block)],
        NN,
        precision=lax.Precision.HIGHEST,
        preferred_element_type=jnp.float32,
    )


def middle_kernel(rows_all, table, gram, image, rounded, out):
    inverse = inverse_factor(gram[...] * (1.0 / rows_all))

    def one(block, _):
        rounded[:, columns_of(block)] = solve_into(inverse, image, block).astype(jnp.bfloat16)
        return 0

    lax.fori_loop(0, image.shape[1] // BLK, one, 0)
    spread(table, rounded, out)


def middle(rows_all, table, gram, image, peer_count):
    return pl.pallas_call(
        functools.partial(middle_kernel, rows_all),
        in_specs=[SMEM, VMEM, VMEM],
        out_specs=[VMEM, VMEM],
        out_shape=[
            jax.ShapeDtypeStruct(image.shape, jnp.bfloat16),
            jax.ShapeDtypeStruct((peer_count, VECS, BLK), jnp.bfloat16),
        ],
        compiler_params=params(),
        cost_estimate=cost(10**8, 4 * 2**20),
        name="middle",
    )(table, gram, image)


def last_kernel(rows_all, gram, image, vectors):
    inverse = inverse_factor(gram[...] * (1.0 / rows_all))

    def one(block, _):
        vectors[:, columns_of(block)] = solve_into(inverse, image, block)
        return 0

    lax.fori_loop(0, image.shape[1] // BLK, one, 0)


def last(rows_all, gram, image):
    return pl.pallas_call(
        functools.partial(last_kernel, rows_all),
        in_specs=[VMEM, VMEM],
        out_specs=VMEM,
        out_shape=jax.ShapeDtypeStruct(image.shape, jnp.float32),
        compiler_params=params(),
        cost_estimate=cost(10**8, 4 * 2**20),
        name="last",
    )(gram, image)


def sum_everywhere(part):
    for axis, masks in (("gy", (1,)), ("gy", (2, 4, 6)), ("gy", (8, 16, 24)), ("gx", (1, 2, 3))):
        size = lax.axis_size(axis)
        arrived = [lax.ppermute(part, axis, [(i, i ^ mask) for i in range(size)]) for mask in masks]
        part = sum(arrived, part)
    return part


def exchange(blocks):
    return lax.all_to_all(blocks, "gy", split_axis=0, concat_axis=0, tiled=True)


def per_device(embeddings, start, requests, pairs, counts):
    peer_count = lax.axis_size("gy")
    rows_all = embeddings.shape[0] * lax.axis_size("gx") * peer_count
    units, send_rows, table = prepare(embeddings, pairs[0], counts, peer_count)
    far_rows = exchange(send_rows)
    wanted = exchange(requests.reshape(peer_count, 1))[:, 0]
    rounded, send_vecs = first_vectors(table, start, peer_count)
    own, local_tiles = local_build(table, units, rounded)
    far_vecs = exchange(send_vecs)
    back, far_tiles = far_build(wanted, units, far_rows, rounded)
    for iteration in range(ITERS):
        if iteration > 0:
            rounded, send_vecs = middle(rows_all, table, gram, image, peer_count)
            far_vecs = exchange(send_vecs)
            back = far_back(wanted, far_tiles, rounded)
            own = local_apply(table, local_tiles, rounded)
        returned = exchange(back)
        own = far_own(wanted, far_tiles, far_vecs, own)
        image, gram = assemble(table, own, returned)
        gram = sum_everywhere(gram)
    return last(rows_all, gram, image)


def solution(mesh):
    return jax.shard_map(
        per_device,
        mesh=mesh,
        in_specs=(
            P(("gx", "gy"), None),
            P(None, ("gx", "gy")),
            P(("gx", "gy"), None),
            P(("gx", "gy"), None, None),
            P(("gx", "gy")),
        ),
        out_specs=P(None, ("gx", "gy")),
        check_vma=False,
    )
```

```python
import functools

import jax
import jax.numpy as jnp
from jax import lax
from jax.experimental import pallas as pl
from jax.experimental.pallas import tpu as pltpu
from jax.sharding import PartitionSpec as P

D = 256
VECS = 32
BLK = 512
ITERS = 2
HALF = BLK // 2
EXTRA = 9

FAR_ROW = 0
LOCAL = 32
LOCAL_COUNT = 96
TABLE = 128

NT = (((1,), (1,)), ((), ()))
NN = (((1,), (0,)), ((), ()))
SMEM = pl.BlockSpec(memory_space=pltpu.SMEM)
VMEM = pl.BlockSpec(memory_space=pltpu.VMEM)
HBM = pl.BlockSpec(memory_space=pltpu.HBM)
GROUP = 4
CHUNK = 2048
VEC_ROWS = 2 * VECS
NOTE_ROWS = 16
PACK = 8
NOTE = BLK + VEC_ROWS
SENT = NOTE + NOTE_ROWS


def in_hbm(array):
    return pltpu.with_memory_space_constraint(array, pltpu.HBM)


def columns_of(block):
    return pl.ds(pl.multiple_of(block * BLK, BLK), BLK)


def params(limit_mib):
    return pltpu.CompilerParams(vmem_limit_bytes=limit_mib * 1024 * 1024)


def cost(flops, bytes_accessed):
    return pl.CostEstimate(flops=flops, bytes_accessed=bytes_accessed, transcendentals=0)


def normalized(rows):
    values = rows.astype(jnp.float32)
    scaled = values * lax.rsqrt(jnp.sum(values * values, axis=-1, keepdims=True) + 1e-06)
    return scaled.astype(jnp.bfloat16)


def note_slots(pairs, counts, table, head, following, block_count):
    def clear(i, _):
        table[FAR_ROW + i] = -1
        head[i] = -1
        return 0

    lax.fori_loop(0, following.shape[0], clear, 0)

    def note(k, local_count):
        row = pairs[0, k]
        col = pairs[1, k]
        far = col >= block_count

        @pl.when(far)
        def _():
            peer = col - block_count
            table[FAR_ROW + peer] = row
            following[peer] = head[row]
            head[row] = peer

        @pl.when(jnp.logical_not(far))
        def _():
            table[LOCAL + local_count] = row * 64 + col

        return local_count + jnp.where(far, 0, 1)

    table[LOCAL_COUNT] = lax.fori_loop(0, counts[0], note, 0)


def prepare_kernel(
    pairs, counts, requests, raw, start, send, rounded, table,
    fresh, vecs, held, notes, head, following, load_sem, vec_sem, note_sem, send_sem,
):
    block_count = held.shape[0]
    peer_count = send.shape[0]

    def load(b):
        return pltpu.make_async_copy(raw.at[pl.ds(b * BLK, BLK), :], fresh.at[b], load_sem.at[b])

    def give(peer, b):
        return pltpu.make_async_copy(held.at[b], send.at[peer, pl.ds(0, NOTE), :], send_sem.at[peer])

    load(0).start()
    vec_load = pltpu.make_async_copy(start, vecs, vec_sem)
    vec_load.start()

    def begin(b, _):
        load(b).start()
        return 0

    lax.fori_loop(1, block_count, begin, 0)
    note_slots(pairs, counts, table, head, following, block_count)

    def write_note(peer, _):
        block = requests[0, peer].astype(jnp.float32)
        notes[peer] = jnp.full((NOTE_ROWS, D), block, jnp.float32).astype(jnp.bfloat16)
        return 0

    lax.fori_loop(0, peer_count, write_note, 0)
    note = pltpu.make_async_copy(notes, send.at[:, pl.ds(NOTE, NOTE_ROWS), :], note_sem)
    note.start()
    vec_load.wait()

    def one(b, _):
        load(b).wait()
        held[b, 0:BLK, :] = normalized(fresh[b])
        w = vecs[:, columns_of(b)].astype(jnp.bfloat16)
        rounded[:, columns_of(b)] = w
        held[b, BLK : BLK + VECS, :] = w[:, :HALF]
        held[b, BLK + VECS : NOTE, :] = w[:, HALF:]

        def emit(peer):
            give(peer, b).start()
            return following[peer]

        lax.while_loop(lambda peer: peer >= 0, emit, head[b])
        return 0

    lax.fori_loop(0, block_count, one, 0)

    def given(peer, _):
        row = table[FAR_ROW + peer]

        @pl.when(row >= 0)
        def _():
            give(peer, row).wait()

        return 0

    lax.fori_loop(0, peer_count, given, 0)
    note.wait()


def prepare(embeddings, start, requests, pairs, counts):
    peer_count = requests.shape[1]
    block_count = embeddings.shape[0] // BLK
    lists = max(block_count, peer_count)
    return pl.pallas_call(
        prepare_kernel,
        in_specs=[SMEM, SMEM, SMEM, HBM, HBM],
        out_specs=[HBM, VMEM, SMEM],
        out_shape=[
            pltpu.HBM((peer_count, SENT, D), jnp.bfloat16),
            jax.ShapeDtypeStruct(start.shape, jnp.bfloat16),
            jax.ShapeDtypeStruct((TABLE,), jnp.int32),
        ],
        scratch_shapes=[
            pltpu.VMEM((block_count, BLK, D), jnp.bfloat16),
            pltpu.VMEM(start.shape, jnp.float32),
            pltpu.VMEM((block_count, NOTE, D), jnp.bfloat16),
            pltpu.VMEM((peer_count, NOTE_ROWS, D), jnp.bfloat16),
            pltpu.SMEM((lists,), jnp.int32),
            pltpu.SMEM((lists,), jnp.int32),
            pltpu.SemaphoreType.DMA((block_count,)),
            pltpu.SemaphoreType.DMA,
            pltpu.SemaphoreType.DMA,
            pltpu.SemaphoreType.DMA((peer_count,)),
        ],
        compiler_params=params(20),
        cost_estimate=cost(10**7, 24 * 2**20),
        name="prepare",
    )(pairs, counts, requests, in_hbm(embeddings), in_hbm(start))


def tile_of(left, right):
    product = lax.dot_general(left, right, NT, preferred_element_type=jnp.float32)
    return (product * product * product).astype(jnp.bfloat16)


def dot_nt(vecs, tile):
    return lax.dot_general(vecs, tile, NT, preferred_element_type=jnp.float32)


def dot_nn(vecs, tile):
    return lax.dot_general(vecs, tile, NN, preferred_element_type=jnp.float32)


def local_build_kernel(
    table, raw, rounded, all_units, total, tiles, done, fresh, units, buffer, sem, unit_sem, keep_sem
):
    block_count = units.shape[0]
    load = pltpu.make_async_copy(raw, fresh, unit_sem)
    load.start()
    count = table[LOCAL_COUNT]
    done[0] = count
    total[...] = jnp.zeros_like(total)
    load.wait()

    def normalize(b, _):
        units[b] = normalized(fresh[pl.ds(pl.multiple_of(b * BLK, BLK), BLK), :])
        return 0

    lax.fori_loop(0, block_count, normalize, 0)
    keep = pltpu.make_async_copy(units, all_units, keep_sem)
    keep.start()

    def copy(n):
        return pltpu.make_async_copy(buffer.at[n % 2], tiles.at[n], sem.at[n % 2])

    def one(n, _):
        code = table[LOCAL + n]
        row = code // 64
        col = code % 64

        @pl.when(n >= 2)
        def _():
            copy(n - 2).wait()

        tile = buffer.at[n % 2]
        tile[...] = tile_of(units[row], units[col])
        copy(n).start()
        total[:, columns_of(col)] += dot_nn(rounded[:, columns_of(row)], tile[...])

        @pl.when(row != col)
        def _():
            total[:, columns_of(row)] += dot_nt(rounded[:, columns_of(col)], tile[...])

        return 0

    lax.fori_loop(0, count, one, 0)

    @pl.when(count >= 2)
    def _():
        copy(count - 2).wait()

    @pl.when(count >= 1)
    def _():
        copy(count - 1).wait()

    keep.wait()


def local_build(table, raw, rounded):
    block_count = raw.shape[0] // BLK
    return pl.pallas_call(
        local_build_kernel,
        in_specs=[SMEM, HBM, VMEM],
        out_specs=[HBM, VMEM, HBM, SMEM],
        out_shape=[
            pltpu.HBM((block_count, BLK, D), jnp.bfloat16),
            jax.ShapeDtypeStruct(rounded.shape, jnp.float32),
            pltpu.HBM((block_count + EXTRA, BLK, BLK), jnp.bfloat16),
            jax.ShapeDtypeStruct((1,), jnp.int32),
        ],
        scratch_shapes=[
            pltpu.VMEM(raw.shape, jnp.bfloat16),
            pltpu.VMEM((block_count, BLK, D), jnp.bfloat16),
            pltpu.VMEM((2, BLK, BLK), jnp.bfloat16),
            pltpu.SemaphoreType.DMA((2,)),
            pltpu.SemaphoreType.DMA,
            pltpu.SemaphoreType.DMA,
        ],
        compiler_params=params(20),
        cost_estimate=cost(33 * 2 * BLK * BLK * (D + 8 * VECS), 32 * 2**20),
        name="local_build",
    )(table, in_hbm(raw), rounded)


def note_active(wanted, active):
    def one(peer, count):
        @pl.when(wanted[peer] >= 0)
        def _():
            active[count] = peer

        return count + jnp.where(wanted[peer] >= 0, 1, 0)

    return lax.fori_loop(0, wanted.shape[0], one, 0)


def build_groups(count, active, wanted, units, far_rows, near, far, buffer, load_sem, use, save=None):
    def loads(n):
        peer = active[n]
        return (
            pltpu.make_async_copy(far_rows.at[peer, pl.ds(0, BLK), :], far.at[n], load_sem.at[0, n]),
            pltpu.make_async_copy(units.at[wanted[peer]], near.at[n], load_sem.at[1, n]),
        )

    def begin(n):
        @pl.when(n < count)
        def _():
            for load in loads(n):
                load.start()

    def group(first, base):
        for z in range(GROUP):
            begin(first + 2 * GROUP + z)
        for z in range(GROUP):

            @pl.when(first + z < count)
            def _(n=first + z):
                for load in loads(n):
                    load.wait()

        if save:

            @pl.when(first >= 2 * GROUP)
            def _():
                for z in range(GROUP):
                    save(first - 2 * GROUP + z, base + z).wait()

        held = [jnp.minimum(first + z, count - 1) for z in range(GROUP)]
        live = [first + z < count for z in range(GROUP)]
        for z, n in enumerate(held):
            buffer[base + z] = tile_of(near[n], far[n])
        use([active[n] for n in held], live, [buffer.at[base + z] for z in range(GROUP)])
        if save:
            for z in range(GROUP):

                @pl.when(live[z])
                def _(n=first + z, z=z):
                    save(n, base + z).start()

    def two_groups(i, _):
        first = 2 * GROUP * i
        group(first, 0)

        @pl.when(first + GROUP < count)
        def _():
            group(first + GROUP, GROUP)

        return 0

    for n in range(2 * GROUP):
        begin(n)
    lax.fori_loop(0, (count + 2 * GROUP - 1) // (2 * GROUP), two_groups, 0)
    if save:
        for z in range(2 * GROUP):
            newest = z + 2 * GROUP * ((count - 1 - z) // (2 * GROUP))

            @pl.when((count > z) & (newest // GROUP * GROUP + 2 * GROUP >= count))
            def _(n=newest, z=z):
                save(n, z).wait()


def build_scratch(peer_count):
    return [
        pltpu.SMEM((peer_count,), jnp.int32),
        pltpu.VMEM((peer_count, BLK, D), jnp.bfloat16),
        pltpu.VMEM((peer_count, BLK, D), jnp.bfloat16),
        pltpu.VMEM((2 * GROUP, BLK, BLK), jnp.bfloat16),
        pltpu.SemaphoreType.DMA((2, peer_count)),
    ]


def far_build_kernel(wanted, units, far_rows, rounded, after, back, active, near, far, buffer, load_sem):
    del after
    count = note_active(wanted, active)

    def use(peers, live, group):
        for peer, tile in zip(peers, group):
            vecs = rounded[:, columns_of(wanted[peer])]
            back[peer] = dot_nn(vecs, tile[...]).astype(jnp.bfloat16)

    build_groups(count, active, wanted, units, far_rows, near, far, buffer, load_sem, use)


def far_build(wanted, units, far_rows, rounded, after):
    peer_count = far_rows.shape[0]
    return pl.pallas_call(
        far_build_kernel,
        in_specs=[SMEM, HBM, HBM, VMEM, SMEM],
        out_specs=VMEM,
        out_shape=jax.ShapeDtypeStruct((peer_count, VECS, BLK), jnp.bfloat16),
        scratch_shapes=build_scratch(peer_count),
        compiler_params=params(28),
        cost_estimate=cost(32 * 2 * BLK * BLK * (D + 4 * VECS), 18 * 2**20),
        name="far_build",
    )(wanted, in_hbm(units), in_hbm(far_rows), rounded, after)


def far_first_kernel(
    wanted, units, far_rows, before, total, tiles,
    active, near, far, buffer, load_sem, vecs, save_sem, vec_sem, before_sem,
):
    count = note_active(wanted, active)
    vec_load = pltpu.make_async_copy(far_rows.at[:, pl.ds(BLK, VEC_ROWS), :], vecs, vec_sem)
    before_load = pltpu.make_async_copy(before, total, before_sem)
    vec_load.start()
    before_load.start()

    def save(n, z):
        return pltpu.make_async_copy(buffer.at[z], tiles.at[active[n]], save_sem.at[z])

    def use(peers, live, group):
        terms = []
        for peer, alive, tile in zip(peers, live, group):
            both = vecs[peer]
            both = masked(alive, jnp.concatenate([both[:VECS], both[VECS:]], axis=1))
            terms.append(dot_nt(both, tile[...]))
        for peer, term in zip(peers, terms):
            total[:, columns_of(wanted[peer])] += term

    vec_load.wait()
    before_load.wait()
    build_groups(count, active, wanted, units, far_rows, near, far, buffer, load_sem, use, save)


def far_first(wanted, units, far_rows, before):
    peer_count = far_rows.shape[0]
    return pl.pallas_call(
        far_first_kernel,
        in_specs=[SMEM, HBM, HBM, HBM],
        out_specs=[VMEM, HBM],
        out_shape=[
            jax.ShapeDtypeStruct(before.shape, jnp.float32),
            pltpu.HBM((peer_count, BLK, BLK), jnp.bfloat16),
        ],
        scratch_shapes=[
            *build_scratch(peer_count),
            pltpu.VMEM((peer_count, VEC_ROWS, D), jnp.bfloat16),
            pltpu.SemaphoreType.DMA((2 * GROUP,)),
            pltpu.SemaphoreType.DMA,
            pltpu.SemaphoreType.DMA,
        ],
        compiler_params=params(28),
        cost_estimate=cost(32 * 2 * BLK * BLK * (D + 4 * VECS), 36 * 2**20),
        name="far_first",
    )(wanted, in_hbm(units), in_hbm(far_rows), in_hbm(before))


def stream(count, source_of, buffer, sem, use):
    slots = 2 * GROUP

    def load(n):
        return pltpu.make_async_copy(source_of(n), buffer.at[n % slots], sem.at[n % slots])

    def begin(n):
        @pl.when(n < count)
        def _():
            load(n).start()

    for n in range(GROUP):
        begin(n)

    def group(g, _):
        first = g * GROUP
        for z in range(GROUP):
            begin(first + GROUP + z)
        for z in range(GROUP):

            @pl.when(first + z < count)
            def _(n=first + z):
                load(n).wait()

        held = [jnp.minimum(first + z, count - 1) for z in range(GROUP)]
        live = [first + z < count for z in range(GROUP)]
        use(held, live, [buffer.at[n % slots] for n in held])
        return 0

    lax.fori_loop(0, (count + GROUP - 1) // GROUP, group, 0)


def tile_scratch():
    return [
        pltpu.VMEM((2 * GROUP, BLK, BLK), jnp.bfloat16),
        pltpu.SemaphoreType.DMA((2 * GROUP,)),
    ]


def masked(live, vecs):
    return jnp.where(live, vecs, jnp.zeros_like(vecs))


def far_back_kernel(wanted, tiles, rounded, back, active, buffer, sem):
    count = note_active(wanted, active)

    def use(held, live, group):
        peers = [active[n] for n in held]
        terms = [
            dot_nn(rounded[:, columns_of(wanted[peer])], tile[...]) for peer, tile in zip(peers, group)
        ]
        for peer, term in zip(peers, terms):
            back[peer] = term.astype(jnp.bfloat16)

    stream(count, lambda n: tiles.at[active[n]], buffer, sem, use)


def far_back(wanted, tiles, rounded):
    peer_count = tiles.shape[0]
    return pl.pallas_call(
        far_back_kernel,
        in_specs=[SMEM, HBM, VMEM],
        out_specs=VMEM,
        out_shape=jax.ShapeDtypeStruct((peer_count, VECS, BLK), jnp.bfloat16),
        scratch_shapes=[pltpu.SMEM((peer_count,), jnp.int32), *tile_scratch()],
        compiler_params=params(12),
        cost_estimate=cost(32 * 2 * BLK * BLK * 4 * VECS, 17 * 2**20),
        name="far_back",
    )(wanted, in_hbm(tiles), rounded)


def add_far(wanted, tiles, vecs_of, before, total, active, buffer, sem):
    count = note_active(wanted, active)
    total[...] = before[...]

    def use(held, live, group):
        peers = [active[n] for n in held]
        terms = [
            dot_nt(masked(alive, vecs_of(peer)), tile[...])
            for peer, alive, tile in zip(peers, live, group)
        ]
        for peer, term in zip(peers, terms):
            total[:, columns_of(wanted[peer])] += term

    stream(count, lambda n: tiles.at[active[n]], buffer, sem, use)


def far_next_kernel(wanted, tiles, far_vecs, before, total, active, buffer, sem):
    add_far(wanted, tiles, lambda peer: far_vecs[peer], before, total, active, buffer, sem)


def far_next(wanted, tiles, far_vecs, before):
    peer_count = tiles.shape[0]
    return pl.pallas_call(
        far_next_kernel,
        in_specs=[SMEM, HBM, VMEM, VMEM],
        out_specs=VMEM,
        out_shape=jax.ShapeDtypeStruct(before.shape, jnp.float32),
        scratch_shapes=[pltpu.SMEM((peer_count,), jnp.int32), *tile_scratch()],
        compiler_params=params(14),
        cost_estimate=cost(32 * 2 * BLK * BLK * 4 * VECS, 20 * 2**20),
        name="far_next",
    )(wanted, in_hbm(tiles), far_vecs, before)


def local_apply_kernel(table, tiles, rounded, total, buffer, sem):
    total[...] = jnp.zeros_like(total)

    def use(held, live, group):
        codes = [table[LOCAL + n] for n in held]
        terms = [
            dot_nn(masked(alive, rounded[:, columns_of(code // 64)]), tile[...])
            for code, alive, tile in zip(codes, live, group)
        ]
        for code, term in zip(codes, terms):
            total[:, columns_of(code % 64)] += term
        for code, alive, tile in zip(codes, live, group):
            row = code // 64
            col = code % 64

            @pl.when(alive & (row != col))
            def _(row=row, col=col, tile=tile):
                total[:, columns_of(row)] += dot_nt(rounded[:, columns_of(col)], tile[...])

    stream(table[LOCAL_COUNT], lambda n: tiles.at[n], buffer, sem, use)


def local_apply(table, tiles, rounded):
    return pl.pallas_call(
        local_apply_kernel,
        in_specs=[SMEM, HBM, VMEM],
        out_specs=VMEM,
        out_shape=jax.ShapeDtypeStruct(rounded.shape, jnp.float32),
        scratch_shapes=tile_scratch(),
        compiler_params=params(12),
        cost_estimate=cost(33 * 2 * BLK * BLK * 8 * VECS, 18 * 2**20),
        name="local_apply",
    )(table, in_hbm(tiles), rounded)


def three_parts(values):
    high = values.astype(jnp.bfloat16)
    rest = values - high.astype(jnp.float32)
    middle = rest.astype(jnp.bfloat16)
    low = (rest - middle.astype(jnp.float32)).astype(jnp.bfloat16)
    return high, middle, low


def factor_parts(factor):
    high, middle, low = three_parts(factor)
    return jnp.concatenate([high, high, high, middle, middle, low], axis=1)


def solved(factor, values):
    high, middle, low = three_parts(values)
    return dot_nn(factor, jnp.concatenate([high, middle, low, high, middle, high], axis=0))


def products(values):
    parts = jnp.concatenate(three_parts(values), axis=0)
    return dot_nt(parts, parts)


def assemble_kernel(table, own, returned, image, gram):
    image[...] = own[...]

    def add(peer, _):
        row = table[FAR_ROW + peer]

        @pl.when(row >= 0)
        def _():
            image[:, columns_of(row)] += returned[peer].astype(jnp.float32)

        return 0

    lax.fori_loop(0, returned.shape[0], add, 0)
    total = jnp.zeros((3 * VECS, 3 * VECS), jnp.float32)
    for c in range(0, image.shape[1], CHUNK):
        total += products(image[:, c : c + CHUNK])
    total = total[:VECS] + total[VECS : 2 * VECS] + total[2 * VECS :]
    total = total[:, :VECS] + total[:, VECS : 2 * VECS] + total[:, 2 * VECS :]
    gram[...] = jnp.concatenate([total[r : r + PACK] for r in range(0, VECS, PACK)], axis=1)


def assemble(table, own, returned):
    return pl.pallas_call(
        assemble_kernel,
        in_specs=[SMEM, VMEM, VMEM],
        out_specs=[VMEM, VMEM],
        out_shape=[
            jax.ShapeDtypeStruct(own.shape, jnp.float32),
            jax.ShapeDtypeStruct((PACK, VECS * VECS // PACK), jnp.float32),
        ],
        compiler_params=params(10),
        cost_estimate=cost(10**8, 5 * 2**20),
        name="assemble",
    )(table, own, returned)


def inverse_factor(matrix):
    both = (VECS, 2 * VECS)
    rows = lax.broadcasted_iota(jnp.int32, both, 0)
    lanes = lax.broadcasted_iota(jnp.int32, both, 1)
    work = jnp.where(
        lanes < VECS,
        jnp.concatenate([matrix, matrix], axis=1),
        jnp.where(rows + VECS == lanes, 1.0, 0.0),
    )
    for k in range(0, VECS, 2):
        first_col = jnp.broadcast_to(work[:, k : k + 1], both)
        next_col = jnp.broadcast_to(work[:, k + 1 : k + 2], both)
        scale = lax.rsqrt(first_col[k : k + 1])
        first_row = work[k : k + 1] * scale
        cross = next_col[k : k + 1] * scale
        next_scale = lax.rsqrt(next_col[k + 1 : k + 2] - cross * cross)
        next_row = (work[k + 1 : k + 2] - cross * first_row) * next_scale
        first_factor = first_col * scale
        next_factor = (next_col - first_factor * cross) * next_scale
        rest = work - (first_factor * first_row + next_factor * next_row)
        kept = jnp.where(rows == k, first_row, jnp.where(rows == k + 1, next_row, work))
        work = jnp.where(rows > k + 1, rest, kept)
    return work[:, VECS:]


def summed_inverse(rows_all, grams):
    packed = jnp.sum(grams[...], axis=0)
    gram = jnp.concatenate([packed[:, c : c + VECS] for c in range(0, packed.shape[1], VECS)], axis=0)
    return factor_parts(inverse_factor(gram * (1.0 / rows_all)))


def middle_kernel(rows_all, table, grams, image, rounded, out):
    factor = summed_inverse(rows_all, grams)
    for c in range(0, image.shape[1], CHUNK):
        rounded[:, c : c + CHUNK] = solved(factor, image[:, c : c + CHUNK]).astype(jnp.bfloat16)

    def give(peer, _):
        row = table[FAR_ROW + peer]

        @pl.when(row >= 0)
        def _():
            out[peer] = rounded[:, columns_of(row)]

        return 0

    lax.fori_loop(0, out.shape[0], give, 0)


def middle(rows_all, table, grams, image):
    return pl.pallas_call(
        functools.partial(middle_kernel, rows_all),
        in_specs=[SMEM, VMEM, VMEM],
        out_specs=[VMEM, VMEM],
        out_shape=[
            jax.ShapeDtypeStruct(image.shape, jnp.bfloat16),
            jax.ShapeDtypeStruct((grams.shape[0], VECS, BLK), jnp.bfloat16),
        ],
        compiler_params=params(10),
        cost_estimate=cost(10**8, 4 * 2**20),
        name="middle",
    )(table, grams, image)


def last_kernel(rows_all, grams, image, vectors):
    factor = summed_inverse(rows_all, grams)
    for c in range(0, image.shape[1], CHUNK):
        vectors[:, c : c + CHUNK] = solved(factor, image[:, c : c + CHUNK])


def last(rows_all, grams, image):
    return pl.pallas_call(
        functools.partial(last_kernel, rows_all),
        in_specs=[VMEM, VMEM],
        out_specs=VMEM,
        out_shape=jax.ShapeDtypeStruct(image.shape, jnp.float32),
        compiler_params=params(10),
        cost_estimate=cost(10**8, 4 * 2**20),
        name="last",
    )(grams, image)


def all_parts(gram):
    size = lax.axis_size("gx")
    arrived = [
        lax.ppermute(gram, "gx", [(i, i ^ mask) for i in range(size)]) for mask in range(1, size)
    ]
    gram = sum(arrived, gram)
    return exchange(jnp.broadcast_to(gram, (lax.axis_size("gy"), *gram.shape)))


def exchange(blocks):
    return lax.all_to_all(blocks, "gy", split_axis=0, concat_axis=0, tiled=True)


def per_device(embeddings, start, requests, pairs, counts):
    rows_all = embeddings.shape[0] * lax.axis_size("gx") * lax.axis_size("gy")
    send_rows, rounded, table = prepare(embeddings, start, requests, pairs[0].T, counts)
    far_rows = exchange(send_rows)
    units, own, local_tiles, done = local_build(table, embeddings, rounded)
    wanted = far_rows[:, NOTE, 0].astype(jnp.int32)
    returned = exchange(far_build(wanted, units, far_rows, rounded, done))
    own, far_tiles = far_first(wanted, units, far_rows, own)
    for _ in range(ITERS - 1):
        image, gram = assemble(table, own, returned)
        rounded, send_vecs = middle(rows_all, table, all_parts(gram), image)
        far_vecs = exchange(send_vecs)
        back = far_back(wanted, far_tiles, rounded)
        own = local_apply(table, local_tiles, rounded)
        returned = exchange(back)
        own = far_next(wanted, far_tiles, far_vecs, own)
    image, gram = assemble(table, own, returned)
    return last(rows_all, all_parts(gram), image)


def solution(mesh):
    return jax.shard_map(
        per_device,
        mesh=mesh,
        in_specs=(
            P(("gx", "gy"), None),
            P(None, ("gx", "gy")),
            P(("gx", "gy"), None),
            P(("gx", "gy"), None, None),
            P(("gx", "gy")),
        ),
        out_specs=P(None, ("gx", "gy")),
        check_vma=False,
    )
```

```python
import functools

import jax
import jax.numpy as jnp
from jax import lax
from jax.experimental import pallas as pl
from jax.experimental.pallas import tpu as pltpu
from jax.sharding import PartitionSpec as P

D = 256
VECS = 32
BLK = 512
HALF = BLK // 2
EXTRA = 9

FAR_ROW = 0
LOCAL = 32
LOCAL_COUNT = 96
TABLE = 128

NT = (((1,), (1,)), ((), ()))
NN = (((1,), (0,)), ((), ()))
SMEM = pl.BlockSpec(memory_space=pltpu.SMEM)
VMEM = pl.BlockSpec(memory_space=pltpu.VMEM)
HBM = pl.BlockSpec(memory_space=pltpu.HBM)
GROUP = 4
CHUNK = 2048
VEC_ROWS = 2 * VECS
NOTE_ROWS = 16
PACK = 8
NOTE = BLK + VEC_ROWS
NOTE_BLOCK = (NOTE + 8, D // 2)
LARGEST = 1e12
SENT = NOTE + NOTE_ROWS


def in_hbm(array):
    return pltpu.with_memory_space_constraint(array, pltpu.HBM)


def columns_of(block):
    return pl.ds(pl.multiple_of(block * BLK, BLK), BLK)


def params(limit_mib):
    return pltpu.CompilerParams(vmem_limit_bytes=limit_mib * 1024 * 1024)


def cost(flops, bytes_accessed):
    return pl.CostEstimate(flops=flops, bytes_accessed=bytes_accessed, transcendentals=0)


def three_parts(values):
    high = values.astype(jnp.bfloat16)
    rest = values - high.astype(jnp.float32)
    middle = rest.astype(jnp.bfloat16)
    low = (rest - middle.astype(jnp.float32)).astype(jnp.bfloat16)
    return high, middle, low


def factor_parts(factor):
    high, middle, low = three_parts(factor)
    return jnp.concatenate([high, high, high, middle, middle, low], axis=1)


def solved(factor, values):
    high, middle, low = three_parts(values)
    return dot_nn(factor, jnp.concatenate([high, middle, low, high, middle, high], axis=0))


def product(left, right):
    return solved(factor_parts(left), right)


def products(values):
    parts = jnp.concatenate(three_parts(values), axis=0)
    return dot_nt(parts, parts)


def sum_of_parts(total):
    total = total[:VECS] + total[VECS : 2 * VECS] + total[2 * VECS :]
    return total[:, :VECS] + total[:, VECS : 2 * VECS] + total[:, 2 * VECS :]


def packed(gram):
    return jnp.concatenate([gram[r : r + PACK] for r in range(0, VECS, PACK)], axis=1)


def unpacked(gram):
    return jnp.concatenate([gram[:, c : c + VECS] for c in range(0, gram.shape[1], VECS)], axis=0)


def normalized(rows):
    values = rows.astype(jnp.float32)
    scaled = values * lax.rsqrt(jnp.sum(values * values, axis=-1, keepdims=True) + 1e-06)
    return scaled.astype(jnp.bfloat16)


def note_slots(pairs, counts, table, head, following, block_count):
    def clear(i, _):
        table[FAR_ROW + i] = -1
        head[i] = -1
        return 0

    lax.fori_loop(0, following.shape[0], clear, 0)

    def note(k, local_count):
        row = pairs[0, k]
        col = pairs[1, k]
        far = col >= block_count
        crossed = jnp.logical_not(far) & (row != col)

        @pl.when(far)
        def _():
            peer = col - block_count
            table[FAR_ROW + peer] = row
            following[peer] = head[row]
            head[row] = peer

        @pl.when(crossed)
        def _():
            table[LOCAL + local_count] = row * 64 + col

        return local_count + jnp.where(crossed, 1, 0)

    table[LOCAL_COUNT] = lax.fori_loop(0, counts[0], note, 0)


def prepare_kernel(
    counts, all_pairs, all_requests, raw, start, send, rounded, table,
    pairs, requests, slot_sem, fresh, vecs, held, notes, head, following, load_sem, vec_sem, note_sem, send_sem,
):
    block_count = held.shape[0]
    peer_count = send.shape[0]

    def load(b):
        return pltpu.make_async_copy(raw.at[pl.ds(b * BLK, BLK), :], fresh.at[b], load_sem.at[b])

    def give(peer, b):
        return pltpu.make_async_copy(held.at[b], send.at[peer, pl.ds(0, NOTE), :], send_sem.at[peer])

    slot_loads = (
        pltpu.make_async_copy(all_pairs, pairs, slot_sem.at[0]),
        pltpu.make_async_copy(all_requests, requests, slot_sem.at[1]),
    )
    for slot_load in slot_loads:
        slot_load.start()
    vec_load = pltpu.make_async_copy(start, vecs, vec_sem)
    vec_load.start()
    for slot_load in slot_loads:
        slot_load.wait()
    note_slots(pairs, counts, table, head, following, block_count)

    def begin(b, _):
        @pl.when(head[b] >= 0)
        def _():
            load(b).start()

        return 0

    lax.fori_loop(0, block_count, begin, 0)

    vec_load.wait()
    gram = jnp.zeros((VECS, VECS), jnp.float32)
    for c in range(0, vecs.shape[1], CHUNK):
        w = vecs[:, c : c + CHUNK]
        rounded[:, c : c + CHUNK] = w.astype(jnp.bfloat16)
        w = jnp.clip(w, -LARGEST, LARGEST).astype(jnp.bfloat16)
        gram += dot_nt(w, w)
    high, middle, low = three_parts(packed(gram))

    def write_note(peer, _):
        block = jnp.full(low.shape, requests[0, peer].astype(jnp.float32), jnp.float32)
        notes[peer] = jnp.concatenate(
            [
                jnp.concatenate([high, middle], axis=1),
                jnp.concatenate([low, block.astype(jnp.bfloat16)], axis=1),
            ],
            axis=0,
        )
        return 0

    lax.fori_loop(0, peer_count, write_note, 0)
    note = pltpu.make_async_copy(notes, send.at[:, pl.ds(NOTE, NOTE_ROWS), :], note_sem)
    note.start()

    def one(b, _):
        @pl.when(head[b] >= 0)
        def _():
            load(b).wait()
            held[b, 0:BLK, :] = normalized(fresh[b])
            w = rounded[:, columns_of(b)]
            held[b, BLK : BLK + VECS, :] = w[:, :HALF]
            held[b, BLK + VECS : NOTE, :] = w[:, HALF:]

            def emit(peer):
                give(peer, b).start()
                return following[peer]

            lax.while_loop(lambda peer: peer >= 0, emit, head[b])

        return 0

    lax.fori_loop(0, block_count, one, 0)

    def given(peer, _):
        row = table[FAR_ROW + peer]

        @pl.when(row >= 0)
        def _():
            give(peer, row).wait()

        return 0

    lax.fori_loop(0, peer_count, given, 0)
    note.wait()


def prepare(embeddings, start, requests, pairs, counts):
    peer_count = requests.shape[1]
    block_count = embeddings.shape[0] // BLK
    lists = max(block_count, peer_count)
    return pl.pallas_call(
        prepare_kernel,
        in_specs=[SMEM, HBM, HBM, HBM, HBM],
        out_specs=[HBM, VMEM, SMEM],
        out_shape=[
            pltpu.HBM((peer_count, SENT, D), jnp.bfloat16),
            jax.ShapeDtypeStruct(start.shape, jnp.bfloat16),
            jax.ShapeDtypeStruct((TABLE,), jnp.int32),
        ],
        scratch_shapes=[
            pltpu.SMEM(pairs.shape, jnp.int32),
            pltpu.SMEM(requests.shape, jnp.int32),
            pltpu.SemaphoreType.DMA((2,)),
            pltpu.VMEM((block_count, BLK, D), jnp.bfloat16),
            pltpu.VMEM(start.shape, jnp.float32),
            pltpu.VMEM((block_count, NOTE, D), jnp.bfloat16),
            pltpu.VMEM((peer_count, NOTE_ROWS, D), jnp.bfloat16),
            pltpu.SMEM((lists,), jnp.int32),
            pltpu.SMEM((lists,), jnp.int32),
            pltpu.SemaphoreType.DMA((block_count,)),
            pltpu.SemaphoreType.DMA,
            pltpu.SemaphoreType.DMA,
            pltpu.SemaphoreType.DMA((peer_count,)),
        ],
        compiler_params=params(20),
        cost_estimate=cost(10**7, 24 * 2**20),
        name="prepare",
    )(counts, in_hbm(pairs), in_hbm(requests), in_hbm(embeddings), in_hbm(start))


def tile_of(left, right):
    product = lax.dot_general(left, right, NT, preferred_element_type=jnp.float32)
    return (product * product * product).astype(jnp.bfloat16)


def dot_nt(vecs, tile):
    return lax.dot_general(vecs, tile, NT, preferred_element_type=jnp.float32)


def dot_nn(vecs, tile):
    return lax.dot_general(vecs, tile, NN, preferred_element_type=jnp.float32)


def local_build_kernel(
    table, raw, rounded, all_units, total, tiles, done, fresh, units, buffer, sem, unit_sem, keep_sem
):
    block_count = units.shape[0]
    load = pltpu.make_async_copy(raw, fresh, unit_sem)
    load.start()
    count = block_count + table[LOCAL_COUNT]
    done[0] = count
    total[...] = jnp.zeros_like(total)
    load.wait()

    def normalize(b, _):
        units[b] = normalized(fresh[pl.ds(pl.multiple_of(b * BLK, BLK), BLK), :])
        return 0

    lax.fori_loop(0, block_count, normalize, 0)
    keep = pltpu.make_async_copy(units, all_units, keep_sem)
    keep.start()

    def copy(n):
        return pltpu.make_async_copy(buffer.at[n % 2], tiles.at[n], sem.at[n % 2])

    def one(n, _):
        code = table[LOCAL + jnp.maximum(n - block_count, 0)]
        row = jnp.where(n < block_count, n, code // 64)
        col = jnp.where(n < block_count, n, code % 64)

        @pl.when(n >= 2)
        def _():
            copy(n - 2).wait()

        tile = buffer.at[n % 2]
        tile[...] = tile_of(units[row], units[col])
        copy(n).start()
        total[:, columns_of(col)] += dot_nn(rounded[:, columns_of(row)], tile[...])

        @pl.when(row != col)
        def _():
            total[:, columns_of(row)] += dot_nt(rounded[:, columns_of(col)], tile[...])

        return 0

    lax.fori_loop(0, count, one, 0)

    @pl.when(count >= 2)
    def _():
        copy(count - 2).wait()

    @pl.when(count >= 1)
    def _():
        copy(count - 1).wait()

    keep.wait()


def local_build(table, raw, rounded):
    block_count = raw.shape[0] // BLK
    return pl.pallas_call(
        local_build_kernel,
        in_specs=[SMEM, HBM, VMEM],
        out_specs=[HBM, VMEM, HBM, SMEM],
        out_shape=[
            pltpu.HBM((block_count, BLK, D), jnp.bfloat16),
            jax.ShapeDtypeStruct(rounded.shape, jnp.float32),
            pltpu.HBM((block_count + EXTRA, BLK, BLK), jnp.bfloat16),
            jax.ShapeDtypeStruct((1,), jnp.int32),
        ],
        scratch_shapes=[
            pltpu.VMEM(raw.shape, jnp.bfloat16),
            pltpu.VMEM((block_count, BLK, D), jnp.bfloat16),
            pltpu.VMEM((2, BLK, BLK), jnp.bfloat16),
            pltpu.SemaphoreType.DMA((2,)),
            pltpu.SemaphoreType.DMA,
            pltpu.SemaphoreType.DMA,
        ],
        compiler_params=params(20),
        cost_estimate=cost(33 * 2 * BLK * BLK * (D + 8 * VECS), 32 * 2**20),
        name="local_build",
    )(table, in_hbm(raw), rounded)


def note_active(wanted, active):
    def one(peer, count):
        @pl.when(wanted[peer] >= 0)
        def _():
            active[count] = peer

        return count + jnp.where(wanted[peer] >= 0, 1, 0)

    return lax.fori_loop(0, wanted.shape[0], one, 0)


def build_groups(
    count, active, wanted, units, far_rows, near, far, buffer, load_sem, use, save=None, after_first=()
):
    def loads(n):
        peer = active[n]
        return (
            pltpu.make_async_copy(far_rows.at[peer, pl.ds(0, BLK), :], far.at[n], load_sem.at[0, n]),
            pltpu.make_async_copy(units.at[wanted[peer]], near.at[n], load_sem.at[1, n]),
        )

    def begin(n):
        @pl.when(n < count)
        def _():
            for load in loads(n):
                load.start()

    def group(first, base):
        for z in range(GROUP):
            begin(first + 2 * GROUP + z)
        for z in range(GROUP):

            @pl.when(first + z < count)
            def _(n=first + z):
                for load in loads(n):
                    load.wait()

        if save:

            @pl.when(first >= 2 * GROUP)
            def _():
                for z in range(GROUP):
                    save(first - 2 * GROUP + z, base + z).wait()

        held = [jnp.minimum(first + z, count - 1) for z in range(GROUP)]
        live = [first + z < count for z in range(GROUP)]
        for z, n in enumerate(held):
            buffer[base + z] = tile_of(near[n], far[n])
        use([active[n] for n in held], live, [buffer.at[base + z] for z in range(GROUP)])
        if save:
            for z in range(GROUP):

                @pl.when(live[z])
                def _(n=first + z, z=z):
                    save(n, base + z).start()

    def two_groups(i, _):
        first = 2 * GROUP * i
        group(first, 0)

        @pl.when(first + GROUP < count)
        def _():
            group(first + GROUP, GROUP)

        return 0

    for n in range(2 * GROUP):
        begin(n)
        if n == GROUP - 1:
            for load in after_first:
                load.start()
    lax.fori_loop(0, (count + 2 * GROUP - 1) // (2 * GROUP), two_groups, 0)
    if save:
        for z in range(2 * GROUP):
            newest = z + 2 * GROUP * ((count - 1 - z) // (2 * GROUP))

            @pl.when((count > z) & (newest // GROUP * GROUP + 2 * GROUP >= count))
            def _(n=newest, z=z):
                save(n, z).wait()


def build_scratch(peer_count):
    return [
        pltpu.SMEM((peer_count,), jnp.int32),
        pltpu.VMEM((peer_count, BLK, D), jnp.bfloat16),
        pltpu.VMEM((peer_count, BLK, D), jnp.bfloat16),
        pltpu.VMEM((2 * GROUP, BLK, BLK), jnp.bfloat16),
        pltpu.SemaphoreType.DMA((2, peer_count)),
    ]


def far_build_kernel(
    wanted, units, far_rows, rounded, after, back, gram, active, near, far, buffer, load_sem, notes, note_sem
):
    del after
    load = pltpu.make_async_copy(far_rows.at[:, pl.ds(NOTE, NOTE_ROWS), :], notes, note_sem)
    count = note_active(wanted, active)

    def use(peers, live, group):
        for peer, tile in zip(peers, group):
            vecs = rounded[:, columns_of(wanted[peer])]
            back[peer] = dot_nn(vecs, tile[...]).astype(jnp.bfloat16)

    build_groups(count, active, wanted, units, far_rows, near, far, buffer, load_sem, use, after_first=[load])
    load.wait()
    total = jnp.sum(notes[...].astype(jnp.float32), axis=0)
    half = D // 2
    gram[...] = total[:PACK, :half] + total[:PACK, half:] + total[PACK:, :half]


def far_build(wanted, units, far_rows, rounded, after):
    peer_count = far_rows.shape[0]
    return pl.pallas_call(
        far_build_kernel,
        in_specs=[SMEM, HBM, HBM, VMEM, SMEM],
        out_specs=[VMEM, VMEM],
        out_shape=[
            jax.ShapeDtypeStruct((peer_count, VECS, BLK), jnp.bfloat16),
            jax.ShapeDtypeStruct((PACK, VECS * VECS // PACK), jnp.float32),
        ],
        scratch_shapes=[
            *build_scratch(peer_count),
            pltpu.VMEM((peer_count, NOTE_ROWS, D), jnp.bfloat16),
            pltpu.SemaphoreType.DMA,
        ],
        compiler_params=params(28),
        cost_estimate=cost(32 * 2 * BLK * BLK * (D + 4 * VECS), 18 * 2**20),
        name="far_build",
    )(wanted, in_hbm(units), in_hbm(far_rows), rounded, after)


def far_first_kernel(
    wanted, units, far_rows, before, total, tiles,
    active, near, far, buffer, load_sem, vecs, save_sem, vec_sem, before_sem,
):
    count = note_active(wanted, active)
    vec_load = pltpu.make_async_copy(far_rows.at[:, pl.ds(BLK, VEC_ROWS), :], vecs, vec_sem)
    before_load = pltpu.make_async_copy(before, total, before_sem)
    vec_load.start()
    before_load.start()

    def save(n, z):
        return pltpu.make_async_copy(buffer.at[z], tiles.at[active[n]], save_sem.at[z])

    def use(peers, live, group):
        terms = []
        for peer, alive, tile in zip(peers, live, group):
            both = vecs[peer]
            both = masked(alive, jnp.concatenate([both[:VECS], both[VECS:]], axis=1))
            terms.append(dot_nt(both, tile[...]))
        for peer, term in zip(peers, terms):
            total[:, columns_of(wanted[peer])] += term

    vec_load.wait()
    before_load.wait()
    build_groups(count, active, wanted, units, far_rows, near, far, buffer, load_sem, use, save)


def far_first(wanted, units, far_rows, before):
    peer_count = far_rows.shape[0]
    return pl.pallas_call(
        far_first_kernel,
        in_specs=[SMEM, HBM, HBM, HBM],
        out_specs=[VMEM, HBM],
        out_shape=[
            jax.ShapeDtypeStruct(before.shape, jnp.float32),
            pltpu.HBM((peer_count, BLK, BLK), jnp.bfloat16),
        ],
        scratch_shapes=[
            *build_scratch(peer_count),
            pltpu.VMEM((peer_count, VEC_ROWS, D), jnp.bfloat16),
            pltpu.SemaphoreType.DMA((2 * GROUP,)),
            pltpu.SemaphoreType.DMA,
            pltpu.SemaphoreType.DMA,
        ],
        compiler_params=params(28),
        cost_estimate=cost(32 * 2 * BLK * BLK * (D + 4 * VECS), 36 * 2**20),
        name="far_first",
    )(wanted, in_hbm(units), in_hbm(far_rows), in_hbm(before))


def stream(count, source_of, buffer, sem, use):
    slots = 2 * GROUP

    def load(n):
        return pltpu.make_async_copy(source_of(n), buffer.at[n % slots], sem.at[n % slots])

    def begin(n):
        @pl.when(n < count)
        def _():
            load(n).start()

    for n in range(GROUP):
        begin(n)

    def group(g, _):
        first = g * GROUP
        for z in range(GROUP):
            begin(first + GROUP + z)
        for z in range(GROUP):

            @pl.when(first + z < count)
            def _(n=first + z):
                load(n).wait()

        held = [jnp.minimum(first + z, count - 1) for z in range(GROUP)]
        live = [first + z < count for z in range(GROUP)]
        use(held, live, [buffer.at[n % slots] for n in held])
        return 0

    lax.fori_loop(0, (count + GROUP - 1) // GROUP, group, 0)


def tile_scratch():
    return [
        pltpu.VMEM((2 * GROUP, BLK, BLK), jnp.bfloat16),
        pltpu.SemaphoreType.DMA((2 * GROUP,)),
    ]


def masked(live, vecs):
    return jnp.where(live, vecs, jnp.zeros_like(vecs))


def own_apply_kernel(tiles, rounded, total, done, buffer, sem):
    count = rounded.shape[1] // BLK
    done[0] = count

    def use(held, live, group):
        terms = [dot_nn(rounded[:, columns_of(n)], tile[...]) for n, tile in zip(held, group)]
        for n, term in zip(held, terms):
            total[:, columns_of(n)] = term

    stream(count, lambda n: tiles.at[n], buffer, sem, use)


def own_apply(tiles, rounded):
    return pl.pallas_call(
        own_apply_kernel,
        in_specs=[HBM, VMEM],
        out_specs=[VMEM, SMEM],
        out_shape=[
            jax.ShapeDtypeStruct(rounded.shape, jnp.float32),
            jax.ShapeDtypeStruct((1,), jnp.int32),
        ],
        scratch_shapes=tile_scratch(),
        compiler_params=params(10),
        cost_estimate=cost(24 * 2 * BLK * BLK * 4 * VECS, 13 * 2**20),
        name="own_apply",
    )(in_hbm(tiles), rounded)


def far_back_kernel(wanted, tiles, rounded, after, back, active, buffer, sem):
    del after
    count = note_active(wanted, active)

    def use(held, live, group):
        peers = [active[n] for n in held]
        terms = [
            dot_nn(rounded[:, columns_of(wanted[peer])], tile[...]) for peer, tile in zip(peers, group)
        ]
        for peer, term in zip(peers, terms):
            back[peer] = term.astype(jnp.bfloat16)

    stream(count, lambda n: tiles.at[active[n]], buffer, sem, use)


def far_back(wanted, tiles, rounded, after):
    peer_count = tiles.shape[0]
    return pl.pallas_call(
        far_back_kernel,
        in_specs=[SMEM, HBM, VMEM, SMEM],
        out_specs=VMEM,
        out_shape=jax.ShapeDtypeStruct((peer_count, VECS, BLK), jnp.bfloat16),
        scratch_shapes=[pltpu.SMEM((peer_count,), jnp.int32), *tile_scratch()],
        compiler_params=params(12),
        cost_estimate=cost(32 * 2 * BLK * BLK * 4 * VECS, 17 * 2**20),
        name="far_back",
    )(wanted, in_hbm(tiles), rounded, after)


def rest_apply_kernel(
    table, wanted, local_tiles, far_tiles, rounded, far_vecs, before, total, active, buffer, sem
):
    block_count = rounded.shape[1] // BLK
    count = note_active(wanted, active)
    total[...] = before[...]

    def use_crossed(held, live, group):
        codes = [table[LOCAL + n] for n in held]
        pairs = [(code // 64, code % 64) for code in codes]
        vecs = [[masked(alive, rounded[:, columns_of(b)]) for b in pair] for pair, alive in zip(pairs, live)]
        to_col = [dot_nn(row_vecs, tile[...]) for (row_vecs, _), tile in zip(vecs, group)]
        to_row = [dot_nt(col_vecs, tile[...]) for (_, col_vecs), tile in zip(vecs, group)]
        for (row, col), row_term, col_term in zip(pairs, to_row, to_col):
            total[:, columns_of(col)] += col_term
            total[:, columns_of(row)] += row_term

    def use_far(held, live, group):
        peers = [active[n] for n in held]
        terms = [
            dot_nt(masked(alive, far_vecs[peer]), tile[...])
            for peer, alive, tile in zip(peers, live, group)
        ]
        for peer, term in zip(peers, terms):
            total[:, columns_of(wanted[peer])] += term

    stream(table[LOCAL_COUNT], lambda n: local_tiles.at[block_count + n], buffer, sem, use_crossed)
    stream(count, lambda n: far_tiles.at[active[n]], buffer, sem, use_far)


def rest_apply(table, wanted, local_tiles, far_tiles, rounded, far_vecs, before):
    return pl.pallas_call(
        rest_apply_kernel,
        in_specs=[SMEM, SMEM, HBM, HBM, VMEM, VMEM, VMEM],
        out_specs=VMEM,
        out_shape=jax.ShapeDtypeStruct(before.shape, jnp.float32),
        scratch_shapes=[pltpu.SMEM(wanted.shape, jnp.int32), *tile_scratch()],
        compiler_params=params(12),
        cost_estimate=cost(40 * 2 * BLK * BLK * 4 * VECS, 24 * 2**20),
        name="rest_apply",
    )(table, wanted, in_hbm(local_tiles), in_hbm(far_tiles), rounded, far_vecs, before)


def add_returned(table, own, returned, image):
    image[...] = own[...]

    def add(peer, _):
        row = table[FAR_ROW + peer]

        @pl.when(row >= 0)
        def _():
            image[:, columns_of(row)] += returned[peer].astype(jnp.float32)

        return 0

    lax.fori_loop(0, returned.shape[0], add, 0)


def gram_kernel(image, gram):
    total = jnp.zeros((3 * VECS, 3 * VECS), jnp.float32)
    for c in range(0, image.shape[1], CHUNK):
        total += products(image[:, c : c + CHUNK])
    gram[...] = packed(sum_of_parts(total))


def forward_kernel(table, own, returned, inverse, rounded, gram, send, image, out, sem):
    factor = factor_parts(inverse[...])
    add_returned(table, own, returned, image)
    for c in range(0, image.shape[1], CHUNK):
        based = solved(factor, image[:, c : c + CHUNK])
        image[:, c : c + CHUNK] = based
        rounded[:, c : c + CHUNK] = based.astype(jnp.bfloat16)

    def give(peer, _):
        row = table[FAR_ROW + peer]

        @pl.when(row >= 0)
        def _():
            out[peer] = rounded[:, columns_of(row)]

        return 0

    lax.fori_loop(0, out.shape[0], give, 0)
    save = pltpu.make_async_copy(out, send, sem)
    save.start()
    gram_kernel(image, gram)
    save.wait()


def forward(table, own, returned, inverse):
    return pl.pallas_call(
        forward_kernel,
        in_specs=[SMEM, VMEM, VMEM, VMEM],
        out_specs=[VMEM, VMEM, HBM],
        out_shape=[
            jax.ShapeDtypeStruct(own.shape, jnp.bfloat16),
            jax.ShapeDtypeStruct((PACK, VECS * VECS // PACK), jnp.float32),
            pltpu.HBM(returned.shape, jnp.bfloat16),
        ],
        scratch_shapes=[
            pltpu.VMEM(own.shape, jnp.float32),
            pltpu.VMEM(returned.shape, jnp.bfloat16),
            pltpu.SemaphoreType.DMA,
        ],
        compiler_params=params(12),
        cost_estimate=cost(10**8, 5 * 2**20),
        name="forward",
    )(table, own, returned, inverse)


def assemble_kernel(table, own, returned, image, gram):
    add_returned(table, own, returned, image)
    gram_kernel(image, gram)


def assemble(table, own, returned):
    return pl.pallas_call(
        assemble_kernel,
        in_specs=[SMEM, VMEM, VMEM],
        out_specs=[VMEM, VMEM],
        out_shape=[
            jax.ShapeDtypeStruct(own.shape, jnp.float32),
            jax.ShapeDtypeStruct((PACK, VECS * VECS // PACK), jnp.float32),
        ],
        compiler_params=params(10),
        cost_estimate=cost(10**8, 5 * 2**20),
        name="assemble",
    )(table, own, returned)


def inverse_factor(matrix):
    both = (VECS, 2 * VECS)
    rows = lax.broadcasted_iota(jnp.int32, both, 0)
    lanes = lax.broadcasted_iota(jnp.int32, both, 1)
    work = jnp.where(
        lanes < VECS,
        jnp.concatenate([matrix, matrix], axis=1),
        jnp.where(rows + VECS == lanes, 1.0, 0.0),
    )
    for k in range(0, VECS, 2):
        first_col = jnp.broadcast_to(work[:, k : k + 1], both)
        next_col = jnp.broadcast_to(work[:, k + 1 : k + 2], both)
        scale = lax.rsqrt(first_col[k : k + 1])
        first_row = work[k : k + 1] * scale
        cross = next_col[k : k + 1] * scale
        next_scale = lax.rsqrt(next_col[k + 1 : k + 2] - cross * cross)
        next_row = (work[k + 1 : k + 2] - cross * first_row) * next_scale
        first_factor = first_col * scale
        next_factor = (next_col - first_factor * cross) * next_scale
        rest = work - (first_factor * first_row + next_factor * next_row)
        kept = jnp.where(rows == k, first_row, jnp.where(rows == k + 1, next_row, work))
        work = jnp.where(rows > k + 1, rest, kept)
    return work[:, VECS:]


def identity():
    rows = lax.broadcasted_iota(jnp.int32, (VECS, VECS), 0)
    lanes = lax.broadcasted_iota(jnp.int32, (VECS, VECS), 1)
    return jnp.where(rows == lanes, 1.0, 0.0).astype(jnp.float32)


def basis_kernel(rows_all, gram, inverse):
    eye = identity()
    matrix = unpacked(gram[...]) * (1.0 / rows_all)
    factor = inverse_factor(matrix * (1.0 + 1e-3 * eye))
    usable = jnp.sum(jnp.abs(factor)) < 1e30
    inverse[...] = jnp.where(usable, factor, eye)


def basis(rows_all, gram):
    return pl.pallas_call(
        functools.partial(basis_kernel, rows_all),
        in_specs=[VMEM],
        out_specs=VMEM,
        out_shape=jax.ShapeDtypeStruct((VECS, VECS), jnp.float32),
        compiler_params=params(4),
        cost_estimate=cost(10**6, 10**4),
        name="basis",
    )(gram)


def last_kernel(rows_all, grams, image, vectors):
    both = jnp.sum(grams[...], axis=0) * (1.0 / rows_all)
    first = inverse_factor(unpacked(both[:PACK]))
    turned = lax.dot_general(
        product(first, unpacked(both[PACK:])),
        first,
        NT,
        precision=lax.Precision.HIGHEST,
        preferred_element_type=jnp.float32,
    )
    factor = factor_parts(product(inverse_factor(turned), first))
    for c in range(0, image.shape[1], CHUNK):
        vectors[:, c : c + CHUNK] = solved(factor, image[:, c : c + CHUNK])


def last(rows_all, grams, image):
    return pl.pallas_call(
        functools.partial(last_kernel, rows_all),
        in_specs=[VMEM, VMEM],
        out_specs=VMEM,
        out_shape=jax.ShapeDtypeStruct(image.shape, jnp.float32),
        compiler_params=params(10),
        cost_estimate=cost(10**8, 4 * 2**20),
        name="last",
    )(grams, image)


def sum_over_gx(gram):
    size = lax.axis_size("gx")
    arrived = [
        lax.ppermute(gram, "gx", [(i, i ^ mask) for i in range(size)]) for mask in range(1, size)
    ]
    return sum(arrived, gram)


def all_parts(gram):
    gram = sum_over_gx(gram)
    return exchange(jnp.broadcast_to(gram, (lax.axis_size("gy"), *gram.shape)))


def exchange(blocks):
    return lax.all_to_all(blocks, "gy", split_axis=0, concat_axis=0, tiled=True)


def per_device(embeddings, start, requests, pairs, counts):
    rows_all = embeddings.shape[0] * lax.axis_size("gx") * lax.axis_size("gy")
    send_rows, rounded, table = prepare(embeddings, start, requests, pairs[0].T, counts)
    far_rows = exchange(send_rows)
    units, own, local_tiles, done = local_build(table, embeddings, rounded)
    wanted = far_rows[:, NOTE_BLOCK[0], NOTE_BLOCK[1]].astype(jnp.int32)
    back, start_gram = far_build(wanted, units, far_rows, rounded, done)
    returned = exchange(back)
    inverse = basis(rows_all, sum_over_gx(start_gram))
    own, far_tiles = far_first(wanted, units, far_rows, own)
    rounded, first_gram, send_vecs = forward(table, own, returned, inverse)
    far_vecs = exchange(send_vecs)
    own, done = own_apply(local_tiles, rounded)
    returned = exchange(far_back(wanted, far_tiles, rounded, done))
    own = rest_apply(table, wanted, local_tiles, far_tiles, rounded, far_vecs, own)
    image, next_gram = assemble(table, own, returned)
    grams = all_parts(jnp.concatenate([first_gram, next_gram], axis=0))
    return last(rows_all, grams, image)


def solution(mesh):
    return jax.shard_map(
        per_device,
        mesh=mesh,
        in_specs=(
            P(("gx", "gy"), None),
            P(None, ("gx", "gy")),
            P(("gx", "gy"), None),
            P(("gx", "gy"), None, None),
            P(("gx", "gy")),
        ),
        out_specs=P(None, ("gx", "gy")),
        check_vma=False,
    )
```

```python
import functools

import jax
import jax.numpy as jnp
from jax import lax
from jax.experimental import pallas as pl
from jax.experimental.pallas import tpu as pltpu
from jax.sharding import PartitionSpec as P

D = 256
VECS = 32
BLK = 512
EXTRA = 9

FAR_ROW = 0
LOCAL = 32
LOCAL_COUNT = 96
TABLE = 128

NT = (((1,), (1,)), ((), ()))
NN = (((1,), (0,)), ((), ()))
SMEM = pl.BlockSpec(memory_space=pltpu.SMEM)
VMEM = pl.BlockSpec(memory_space=pltpu.VMEM)
HBM = pl.BlockSpec(memory_space=pltpu.HBM)
GROUP = 4
BUFFERS = 16
CHUNK = 2048
NOTE_ROWS = 16
PACK = 8
NOTE = BLK
NOTE_BLOCK = (NOTE + 8, D // 2)
LARGEST = 1e12
SENT = NOTE + NOTE_ROWS


def in_hbm(array):
    return pltpu.with_memory_space_constraint(array, pltpu.HBM)


def columns_of(block):
    return pl.ds(pl.multiple_of(block * BLK, BLK), BLK)


def params(limit_mib):
    return pltpu.CompilerParams(vmem_limit_bytes=limit_mib * 1024 * 1024)


def cost(flops, bytes_accessed):
    return pl.CostEstimate(flops=flops, bytes_accessed=bytes_accessed, transcendentals=0)


def three_parts(values):
    high = values.astype(jnp.bfloat16)
    rest = values - high.astype(jnp.float32)
    middle = rest.astype(jnp.bfloat16)
    low = (rest - middle.astype(jnp.float32)).astype(jnp.bfloat16)
    return high, middle, low


def factor_parts(factor):
    high, middle, low = three_parts(factor)
    return jnp.concatenate([high, high, high, middle, middle, low], axis=1)


def solved(factor, values):
    high, middle, low = three_parts(values)
    return dot_nn(factor, jnp.concatenate([high, middle, low, high, middle, high], axis=0))


def product(left, right):
    return solved(factor_parts(left), right)


def products(values):
    parts = jnp.concatenate(three_parts(values), axis=0)
    return dot_nt(parts, parts)


def sum_of_parts(total):
    total = total[:VECS] + total[VECS : 2 * VECS] + total[2 * VECS :]
    return total[:, :VECS] + total[:, VECS : 2 * VECS] + total[:, 2 * VECS :]


def packed(gram):
    return jnp.concatenate([gram[r : r + PACK] for r in range(0, VECS, PACK)], axis=1)


def unpacked(gram):
    return jnp.concatenate([gram[:, c : c + VECS] for c in range(0, gram.shape[1], VECS)], axis=0)


def normalized(rows):
    values = rows.astype(jnp.float32)
    scaled = values * lax.rsqrt(jnp.sum(values * values, axis=-1, keepdims=True) + 1e-06)
    return scaled.astype(jnp.bfloat16)


def note_slots(pairs, counts, table, head, following, block_count):
    def clear(i, _):
        table[FAR_ROW + i] = -1
        head[i] = -1
        return 0

    lax.fori_loop(0, following.shape[0], clear, 0)

    def note(k, local_count):
        row = pairs[0, k]
        col = pairs[1, k]
        far = col >= block_count
        crossed = jnp.logical_not(far) & (row != col)

        @pl.when(far)
        def _():
            peer = col - block_count
            table[FAR_ROW + peer] = row
            following[peer] = head[row]
            head[row] = peer

        @pl.when(crossed)
        def _():
            table[LOCAL + local_count] = row * 64 + col

        return local_count + jnp.where(crossed, 1, 0)

    table[LOCAL_COUNT] = lax.fori_loop(0, counts[0], note, 0)


def prepare_kernel(
    counts, all_pairs, all_requests, raw, start, send, rounded, table,
    pairs, requests, slot_sem, fresh, vecs, held, notes, head, following, load_sem, vec_sem, note_sem, send_sem,
):
    block_count = held.shape[0]
    peer_count = send.shape[0]

    def load(b):
        return pltpu.make_async_copy(raw.at[pl.ds(b * BLK, BLK), :], fresh.at[b], load_sem.at[b])

    def give(peer, b):
        return pltpu.make_async_copy(held.at[b], send.at[peer, pl.ds(0, NOTE), :], send_sem.at[peer])

    slot_loads = (
        pltpu.make_async_copy(all_pairs, pairs, slot_sem.at[0]),
        pltpu.make_async_copy(all_requests, requests, slot_sem.at[1]),
    )
    for slot_load in slot_loads:
        slot_load.start()
    vec_load = pltpu.make_async_copy(start, vecs, vec_sem)
    vec_load.start()
    for slot_load in slot_loads:
        slot_load.wait()
    note_slots(pairs, counts, table, head, following, block_count)

    def begin(b, _):
        @pl.when(head[b] >= 0)
        def _():
            load(b).start()

        return 0

    lax.fori_loop(0, block_count, begin, 0)

    vec_load.wait()
    gram = jnp.zeros((VECS, VECS), jnp.float32)
    for c in range(0, vecs.shape[1], CHUNK):
        w = vecs[:, c : c + CHUNK]
        rounded[:, c : c + CHUNK] = w.astype(jnp.bfloat16)
        w = jnp.clip(w, -LARGEST, LARGEST).astype(jnp.bfloat16)
        gram += dot_nt(w, w)
    high, middle, low = three_parts(packed(gram))

    def write_note(peer, _):
        block = jnp.full(low.shape, requests[0, peer].astype(jnp.float32), jnp.float32)
        notes[peer] = jnp.concatenate(
            [
                jnp.concatenate([high, middle], axis=1),
                jnp.concatenate([low, block.astype(jnp.bfloat16)], axis=1),
            ],
            axis=0,
        )
        return 0

    lax.fori_loop(0, peer_count, write_note, 0)
    note = pltpu.make_async_copy(notes, send.at[:, pl.ds(NOTE, NOTE_ROWS), :], note_sem)
    note.start()

    def one(b, _):
        @pl.when(head[b] >= 0)
        def _():
            load(b).wait()
            held[b] = normalized(fresh[b])

            def emit(peer):
                give(peer, b).start()
                return following[peer]

            lax.while_loop(lambda peer: peer >= 0, emit, head[b])

        return 0

    lax.fori_loop(0, block_count, one, 0)

    def given(peer, _):
        row = table[FAR_ROW + peer]

        @pl.when(row >= 0)
        def _():
            give(peer, row).wait()

        return 0

    lax.fori_loop(0, peer_count, given, 0)
    note.wait()


def prepare(embeddings, start, requests, pairs, counts):
    peer_count = requests.shape[1]
    block_count = embeddings.shape[0] // BLK
    lists = max(block_count, peer_count)
    return pl.pallas_call(
        prepare_kernel,
        in_specs=[SMEM, HBM, HBM, HBM, HBM],
        out_specs=[HBM, VMEM, SMEM],
        out_shape=[
            pltpu.HBM((peer_count, SENT, D), jnp.bfloat16),
            jax.ShapeDtypeStruct(start.shape, jnp.bfloat16),
            jax.ShapeDtypeStruct((TABLE,), jnp.int32),
        ],
        scratch_shapes=[
            pltpu.SMEM(pairs.shape, jnp.int32),
            pltpu.SMEM(requests.shape, jnp.int32),
            pltpu.SemaphoreType.DMA((2,)),
            pltpu.VMEM((block_count, BLK, D), jnp.bfloat16),
            pltpu.VMEM(start.shape, jnp.float32),
            pltpu.VMEM((block_count, NOTE, D), jnp.bfloat16),
            pltpu.VMEM((peer_count, NOTE_ROWS, D), jnp.bfloat16),
            pltpu.SMEM((lists,), jnp.int32),
            pltpu.SMEM((lists,), jnp.int32),
            pltpu.SemaphoreType.DMA((block_count,)),
            pltpu.SemaphoreType.DMA,
            pltpu.SemaphoreType.DMA,
            pltpu.SemaphoreType.DMA((peer_count,)),
        ],
        compiler_params=params(20),
        cost_estimate=cost(10**7, 24 * 2**20),
        name="prepare",
    )(counts, in_hbm(pairs), in_hbm(requests), in_hbm(embeddings), in_hbm(start))


def tile_of(left, right):
    product = lax.dot_general(left, right, NT, preferred_element_type=jnp.float32)
    return (product * product * product).astype(jnp.bfloat16)


def dot_nt(vecs, tile):
    return lax.dot_general(vecs, tile, NT, preferred_element_type=jnp.float32)


def dot_nn(vecs, tile):
    return lax.dot_general(vecs, tile, NN, preferred_element_type=jnp.float32)


def local_build_kernel(
    table, raw, rounded, all_units, out, tiles, send, done,
    fresh, units, total, given, buffer, sem, unit_sem, keep_sem, save_sem, send_sem,
):
    block_count = units.shape[0]
    load = pltpu.make_async_copy(raw, fresh, unit_sem)
    load.start()
    count = block_count + table[LOCAL_COUNT]
    done[0] = count
    total[...] = jnp.zeros_like(total)
    spread(table, rounded, given)
    give = pltpu.make_async_copy(given, send, send_sem)
    give.start()
    load.wait()

    def normalize(b, _):
        units[b] = normalized(fresh[pl.ds(pl.multiple_of(b * BLK, BLK), BLK), :])
        return 0

    lax.fori_loop(0, block_count, normalize, 0)
    keep = pltpu.make_async_copy(units, all_units, keep_sem)
    keep.start()

    def copy(n):
        return pltpu.make_async_copy(buffer.at[n % 2], tiles.at[n], sem.at[n % 2])

    def one(n, _):
        code = table[LOCAL + jnp.maximum(n - block_count, 0)]
        row = jnp.where(n < block_count, n, code // 64)
        col = jnp.where(n < block_count, n, code % 64)

        @pl.when(n >= 2)
        def _():
            copy(n - 2).wait()

        tile = buffer.at[n % 2]
        tile[...] = tile_of(units[row], units[col])
        copy(n).start()
        total[:, columns_of(col)] += dot_nn(rounded[:, columns_of(row)], tile[...])

        @pl.when(row != col)
        def _():
            total[:, columns_of(row)] += dot_nt(rounded[:, columns_of(col)], tile[...])

        return 0

    lax.fori_loop(0, count, one, 0)

    @pl.when(count >= 2)
    def _():
        copy(count - 2).wait()

    @pl.when(count >= 1)
    def _():
        copy(count - 1).wait()

    save = pltpu.make_async_copy(total, out, save_sem)
    save.start()
    save.wait()
    keep.wait()
    give.wait()


def local_build(table, raw, rounded, peer_count):
    block_count = raw.shape[0] // BLK
    given = (peer_count, VECS, BLK)
    return pl.pallas_call(
        local_build_kernel,
        in_specs=[SMEM, HBM, VMEM],
        out_specs=[HBM, HBM, HBM, HBM, SMEM],
        out_shape=[
            pltpu.HBM((block_count, BLK, D), jnp.bfloat16),
            pltpu.HBM(rounded.shape, jnp.float32),
            pltpu.HBM((block_count + EXTRA, BLK, BLK), jnp.bfloat16),
            pltpu.HBM(given, jnp.bfloat16),
            jax.ShapeDtypeStruct((1,), jnp.int32),
        ],
        scratch_shapes=[
            pltpu.VMEM(raw.shape, jnp.bfloat16),
            pltpu.VMEM((block_count, BLK, D), jnp.bfloat16),
            pltpu.VMEM(rounded.shape, jnp.float32),
            pltpu.VMEM(given, jnp.bfloat16),
            pltpu.VMEM((2, BLK, BLK), jnp.bfloat16),
            pltpu.SemaphoreType.DMA((2,)),
            pltpu.SemaphoreType.DMA,
            pltpu.SemaphoreType.DMA,
            pltpu.SemaphoreType.DMA,
            pltpu.SemaphoreType.DMA,
        ],
        compiler_params=params(20),
        cost_estimate=cost(33 * 2 * BLK * BLK * (D + 8 * VECS), 32 * 2**20),
        name="local_build",
    )(table, in_hbm(raw), rounded)


def spread(table, source, out):
    def give(peer, _):
        row = table[FAR_ROW + peer]

        @pl.when(row >= 0)
        def _():
            out[peer] = source[:, columns_of(row)]

        return 0

    lax.fori_loop(0, out.shape[0], give, 0)


def note_active(wanted, active):
    def one(peer, count):
        @pl.when(wanted[peer] >= 0)
        def _():
            active[count] = peer

        return count + jnp.where(wanted[peer] >= 0, 1, 0)

    return lax.fori_loop(0, wanted.shape[0], one, 0)


def tile_loads(wanted, active, units, far_rows, near, far, load_sem, n):
    peer = active[n]
    return (
        pltpu.make_async_copy(far_rows.at[peer, pl.ds(0, BLK), :], far.at[n], load_sem.at[0, n]),
        pltpu.make_async_copy(units.at[wanted[peer]], near.at[n], load_sem.at[1, n]),
    )


def far_build_kernel(
    wanted, units, far_rows, rounded, after, back, gram, tiles,
    active, near, far, buffer, load_sem, save_sem, notes, note_sem,
):
    del after
    note_load = pltpu.make_async_copy(far_rows.at[:, pl.ds(NOTE, NOTE_ROWS), :], notes, note_sem)
    count = note_active(wanted, active)
    loads = functools.partial(tile_loads, wanted, active, units, far_rows, near, far, load_sem)

    def save(n, z):
        return pltpu.make_async_copy(buffer.at[z], tiles.at[active[n]], save_sem.at[z])

    def begin(n):
        @pl.when(n < count)
        def _():
            for load in loads(n):
                load.start()

    def group(first, base):
        for z in range(GROUP):
            begin(first + 2 * GROUP + z)
        for z in range(GROUP):

            @pl.when(first + z < count)
            def _(n=first + z):
                for load in loads(n):
                    load.wait()

        @pl.when(first >= 2 * GROUP)
        def _():
            for z in range(GROUP):
                save(first - 2 * GROUP + z, base + z).wait()

        held = [jnp.minimum(first + z, count - 1) for z in range(GROUP)]
        peers = [active[n] for n in held]
        for z, n in enumerate(held):
            buffer[base + z] = tile_of(near[n], far[n])
        for z, peer in enumerate(peers):
            vecs = rounded[:, columns_of(wanted[peer])]
            back[peer] = dot_nn(vecs, buffer[base + z]).astype(jnp.bfloat16)
        for z in range(GROUP):

            @pl.when(first + z < count)
            def _(n=first + z, z=z):
                save(n, base + z).start()

    def two_groups(i, _):
        first = 2 * GROUP * i
        group(first, 0)

        @pl.when(first + GROUP < count)
        def _():
            group(first + GROUP, GROUP)

        return 0

    for n in range(2 * GROUP):
        begin(n)
        if n == GROUP - 1:
            note_load.start()
    lax.fori_loop(0, (count + 2 * GROUP - 1) // (2 * GROUP), two_groups, 0)
    note_load.wait()
    total = jnp.sum(notes[...].astype(jnp.float32), axis=0)
    half = D // 2
    gram[...] = total[:PACK, :half] + total[:PACK, half:] + total[PACK:, :half]
    for z in range(2 * GROUP):
        newest = z + 2 * GROUP * ((count - 1 - z) // (2 * GROUP))

        @pl.when((count > z) & (newest // GROUP * GROUP + 2 * GROUP >= count))
        def _(n=newest, z=z):
            save(n, z).wait()


def far_build(wanted, units, far_rows, rounded, after):
    peer_count = far_rows.shape[0]
    return pl.pallas_call(
        far_build_kernel,
        in_specs=[SMEM, HBM, HBM, VMEM, SMEM],
        out_specs=[VMEM, VMEM, HBM],
        out_shape=[
            jax.ShapeDtypeStruct((peer_count, VECS, BLK), jnp.bfloat16),
            jax.ShapeDtypeStruct((PACK, VECS * VECS // PACK), jnp.float32),
            pltpu.HBM((peer_count, BLK, BLK), jnp.bfloat16),
        ],
        scratch_shapes=[
            pltpu.SMEM((peer_count,), jnp.int32),
            pltpu.VMEM((peer_count, BLK, D), jnp.bfloat16),
            pltpu.VMEM((peer_count, BLK, D), jnp.bfloat16),
            pltpu.VMEM((2 * GROUP, BLK, BLK), jnp.bfloat16),
            pltpu.SemaphoreType.DMA((2, peer_count)),
            pltpu.SemaphoreType.DMA((2 * GROUP,)),
            pltpu.VMEM((peer_count, NOTE_ROWS, D), jnp.bfloat16),
            pltpu.SemaphoreType.DMA,
        ],
        compiler_params=params(28),
        cost_estimate=cost(32 * 2 * BLK * BLK * (D + 4 * VECS), 34 * 2**20),
        name="far_build",
    )(wanted, in_hbm(units), in_hbm(far_rows), rounded, after)


def stream(count, source_of, buffer, sem, use):
    def load(n):
        return pltpu.make_async_copy(source_of(n), buffer.at[n % BUFFERS], sem.at[n % BUFFERS])

    def begin(n):
        @pl.when(n < count)
        def _():
            load(n).start()

    for n in range(BUFFERS - GROUP):
        begin(n)

    def group(g, _):
        first = g * GROUP
        for z in range(GROUP):
            begin(first + BUFFERS - GROUP + z)
        for z in range(GROUP):

            @pl.when(first + z < count)
            def _(n=first + z):
                load(n).wait()

        held = [jnp.minimum(first + z, count - 1) for z in range(GROUP)]
        live = [first + z < count for z in range(GROUP)]
        use(held, live, [buffer.at[n % BUFFERS] for n in held])
        return 0

    lax.fori_loop(0, (count + GROUP - 1) // GROUP, group, 0)


def tile_scratch():
    return [
        pltpu.VMEM((BUFFERS, BLK, BLK), jnp.bfloat16),
        pltpu.SemaphoreType.DMA((BUFFERS,)),
    ]


def masked(live, vecs):
    return jnp.where(live, vecs, jnp.zeros_like(vecs))


def own_apply_kernel(tiles, rounded, out, done, total, buffer, sem, save_sem):
    count = rounded.shape[1] // BLK
    done[0] = count

    def use(held, live, group):
        terms = [dot_nn(rounded[:, columns_of(n)], tile[...]) for n, tile in zip(held, group)]
        for n, term in zip(held, terms):
            total[:, columns_of(n)] = term

    stream(count, lambda n: tiles.at[n], buffer, sem, use)
    save = pltpu.make_async_copy(total, out, save_sem)
    save.start()
    save.wait()


def own_apply(tiles, rounded):
    return pl.pallas_call(
        own_apply_kernel,
        in_specs=[HBM, VMEM],
        out_specs=[HBM, SMEM],
        out_shape=[
            pltpu.HBM(rounded.shape, jnp.float32),
            jax.ShapeDtypeStruct((1,), jnp.int32),
        ],
        scratch_shapes=[
            pltpu.VMEM(rounded.shape, jnp.float32),
            *tile_scratch(),
            pltpu.SemaphoreType.DMA,
        ],
        compiler_params=params(16),
        cost_estimate=cost(24 * 2 * BLK * BLK * 4 * VECS, 13 * 2**20),
        name="own_apply",
    )(in_hbm(tiles), rounded)


def far_back_kernel(wanted, tiles, rounded, after, back, active, buffer, sem):
    del after
    count = note_active(wanted, active)

    def use(held, live, group):
        peers = [active[n] for n in held]
        terms = [
            dot_nn(rounded[:, columns_of(wanted[peer])], tile[...]) for peer, tile in zip(peers, group)
        ]
        for peer, term in zip(peers, terms):
            back[peer] = term.astype(jnp.bfloat16)

    stream(count, lambda n: tiles.at[active[n]], buffer, sem, use)


def far_back(wanted, tiles, rounded, after):
    peer_count = tiles.shape[0]
    return pl.pallas_call(
        far_back_kernel,
        in_specs=[SMEM, HBM, VMEM, SMEM],
        out_specs=VMEM,
        out_shape=jax.ShapeDtypeStruct((peer_count, VECS, BLK), jnp.bfloat16),
        scratch_shapes=[pltpu.SMEM((peer_count,), jnp.int32), *tile_scratch()],
        compiler_params=params(16),
        cost_estimate=cost(32 * 2 * BLK * BLK * 4 * VECS, 17 * 2**20),
        name="far_back",
    )(wanted, in_hbm(tiles), rounded, after)


def add_far(wanted, tiles, far_vecs, total, active, buffer, sem):
    count = note_active(wanted, active)

    def use(held, live, group):
        peers = [active[n] for n in held]
        terms = [
            dot_nt(masked(alive, far_vecs[peer]), tile[...])
            for peer, alive, tile in zip(peers, live, group)
        ]
        for peer, term in zip(peers, terms):
            total[:, columns_of(wanted[peer])] += term

    stream(count, lambda n: tiles.at[active[n]], buffer, sem, use)


def far_first_kernel(wanted, tiles, far_vecs, before, total, active, buffer, sem, before_sem):
    before_load = pltpu.make_async_copy(before, total, before_sem)
    before_load.start()
    before_load.wait()
    add_far(wanted, tiles, far_vecs, total, active, buffer, sem)


def far_first(wanted, tiles, far_vecs, before):
    return pl.pallas_call(
        far_first_kernel,
        in_specs=[SMEM, HBM, VMEM, HBM],
        out_specs=VMEM,
        out_shape=jax.ShapeDtypeStruct(before.shape, jnp.float32),
        scratch_shapes=[
            pltpu.SMEM(wanted.shape, jnp.int32),
            *tile_scratch(),
            pltpu.SemaphoreType.DMA,
        ],
        compiler_params=params(16),
        cost_estimate=cost(32 * 2 * BLK * BLK * 4 * VECS, 20 * 2**20),
        name="far_first",
    )(wanted, in_hbm(tiles), far_vecs, in_hbm(before))


def rest_apply_kernel(
    table, wanted, local_tiles, far_tiles, rounded, far_vecs, before, total, active, buffer, sem, before_sem
):
    block_count = rounded.shape[1] // BLK
    before_load = pltpu.make_async_copy(before, total, before_sem)
    before_load.start()
    before_load.wait()

    def use_crossed(held, live, group):
        codes = [table[LOCAL + n] for n in held]
        pairs = [(code // 64, code % 64) for code in codes]
        vecs = [[masked(alive, rounded[:, columns_of(b)]) for b in pair] for pair, alive in zip(pairs, live)]
        to_col = [dot_nn(row_vecs, tile[...]) for (row_vecs, _), tile in zip(vecs, group)]
        to_row = [dot_nt(col_vecs, tile[...]) for (_, col_vecs), tile in zip(vecs, group)]
        for (row, col), row_term, col_term in zip(pairs, to_row, to_col):
            total[:, columns_of(col)] += col_term
            total[:, columns_of(row)] += row_term

    stream(table[LOCAL_COUNT], lambda n: local_tiles.at[block_count + n], buffer, sem, use_crossed)
    add_far(wanted, far_tiles, far_vecs, total, active, buffer, sem)


def rest_apply(table, wanted, local_tiles, far_tiles, rounded, far_vecs, before):
    return pl.pallas_call(
        rest_apply_kernel,
        in_specs=[SMEM, SMEM, HBM, HBM, VMEM, VMEM, HBM],
        out_specs=VMEM,
        out_shape=jax.ShapeDtypeStruct(before.shape, jnp.float32),
        scratch_shapes=[pltpu.SMEM(wanted.shape, jnp.int32), *tile_scratch(), pltpu.SemaphoreType.DMA],
        compiler_params=params(16),
        cost_estimate=cost(40 * 2 * BLK * BLK * 4 * VECS, 24 * 2**20),
        name="rest_apply",
    )(table, wanted, in_hbm(local_tiles), in_hbm(far_tiles), rounded, far_vecs, in_hbm(before))


def add_returned(table, own, returned, image):
    image[...] = own[...]

    def add(peer, _):
        row = table[FAR_ROW + peer]

        @pl.when(row >= 0)
        def _():
            image[:, columns_of(row)] += returned[peer].astype(jnp.float32)

        return 0

    lax.fori_loop(0, returned.shape[0], add, 0)


def gram_kernel(image, gram):
    total = jnp.zeros((3 * VECS, 3 * VECS), jnp.float32)
    for c in range(0, image.shape[1], CHUNK):
        total += products(image[:, c : c + CHUNK])
    gram[...] = packed(sum_of_parts(total))


def forward_kernel(table, own, returned, inverse, rounded, gram, send, image, out, sem):
    factor = factor_parts(inverse[...])
    add_returned(table, own, returned, image)
    for c in range(0, image.shape[1], CHUNK):
        based = solved(factor, image[:, c : c + CHUNK])
        image[:, c : c + CHUNK] = based
        rounded[:, c : c + CHUNK] = based.astype(jnp.bfloat16)

    spread(table, rounded, out)
    save = pltpu.make_async_copy(out, send, sem)
    save.start()
    gram_kernel(image, gram)
    save.wait()


def forward(table, own, returned, inverse):
    return pl.pallas_call(
        forward_kernel,
        in_specs=[SMEM, VMEM, VMEM, VMEM],
        out_specs=[VMEM, VMEM, HBM],
        out_shape=[
            jax.ShapeDtypeStruct(own.shape, jnp.bfloat16),
            jax.ShapeDtypeStruct((PACK, VECS * VECS // PACK), jnp.float32),
            pltpu.HBM(returned.shape, jnp.bfloat16),
        ],
        scratch_shapes=[
            pltpu.VMEM(own.shape, jnp.float32),
            pltpu.VMEM(returned.shape, jnp.bfloat16),
            pltpu.SemaphoreType.DMA,
        ],
        compiler_params=params(12),
        cost_estimate=cost(10**8, 5 * 2**20),
        name="forward",
    )(table, own, returned, inverse)


def assemble_kernel(table, own, returned, image, gram):
    add_returned(table, own, returned, image)
    gram_kernel(image, gram)


def assemble(table, own, returned):
    return pl.pallas_call(
        assemble_kernel,
        in_specs=[SMEM, VMEM, VMEM],
        out_specs=[VMEM, VMEM],
        out_shape=[
            jax.ShapeDtypeStruct(own.shape, jnp.float32),
            jax.ShapeDtypeStruct((PACK, VECS * VECS // PACK), jnp.float32),
        ],
        compiler_params=params(10),
        cost_estimate=cost(10**8, 5 * 2**20),
        name="assemble",
    )(table, own, returned)


def inverse_factor(matrix):
    both = (VECS, 2 * VECS)
    rows = lax.broadcasted_iota(jnp.int32, both, 0)
    lanes = lax.broadcasted_iota(jnp.int32, both, 1)
    work = jnp.where(
        lanes < VECS,
        jnp.concatenate([matrix, matrix], axis=1),
        jnp.where(rows + VECS == lanes, 1.0, 0.0),
    )
    for k in range(0, VECS, 2):
        first_col = jnp.broadcast_to(work[:, k : k + 1], both)
        next_col = jnp.broadcast_to(work[:, k + 1 : k + 2], both)
        scale = lax.rsqrt(first_col[k : k + 1])
        first_row = work[k : k + 1] * scale
        cross = next_col[k : k + 1] * scale
        next_scale = lax.rsqrt(next_col[k + 1 : k + 2] - cross * cross)
        next_row = (work[k + 1 : k + 2] - cross * first_row) * next_scale
        first_factor = first_col * scale
        next_factor = (next_col - first_factor * cross) * next_scale
        rest = work - (first_factor * first_row + next_factor * next_row)
        kept = jnp.where(rows == k, first_row, jnp.where(rows == k + 1, next_row, work))
        work = jnp.where(rows > k + 1, rest, kept)
    return work[:, VECS:]


def identity():
    rows = lax.broadcasted_iota(jnp.int32, (VECS, VECS), 0)
    lanes = lax.broadcasted_iota(jnp.int32, (VECS, VECS), 1)
    return jnp.where(rows == lanes, 1.0, 0.0).astype(jnp.float32)


def basis_kernel(rows_all, gram, inverse):
    eye = identity()
    matrix = unpacked(gram[...]) * (1.0 / rows_all)
    factor = inverse_factor(matrix * (1.0 + 1e-3 * eye))
    usable = jnp.sum(jnp.abs(factor)) < 1e30
    inverse[...] = jnp.where(usable, factor, eye)


def basis(rows_all, gram):
    return pl.pallas_call(
        functools.partial(basis_kernel, rows_all),
        in_specs=[VMEM],
        out_specs=VMEM,
        out_shape=jax.ShapeDtypeStruct((VECS, VECS), jnp.float32),
        compiler_params=params(4),
        cost_estimate=cost(10**6, 10**4),
        name="basis",
    )(gram)


def last_kernel(rows_all, grams, image, vectors):
    both = jnp.sum(grams[...], axis=0) * (1.0 / rows_all)
    first = inverse_factor(unpacked(both[:PACK]))
    turned = lax.dot_general(
        product(first, unpacked(both[PACK:])),
        first,
        NT,
        precision=lax.Precision.HIGHEST,
        preferred_element_type=jnp.float32,
    )
    factor = factor_parts(product(inverse_factor(turned), first))
    for c in range(0, image.shape[1], CHUNK):
        vectors[:, c : c + CHUNK] = solved(factor, image[:, c : c + CHUNK])


def last(rows_all, grams, image):
    return pl.pallas_call(
        functools.partial(last_kernel, rows_all),
        in_specs=[VMEM, VMEM],
        out_specs=VMEM,
        out_shape=jax.ShapeDtypeStruct(image.shape, jnp.float32),
        compiler_params=params(10),
        cost_estimate=cost(10**8, 4 * 2**20),
        name="last",
    )(grams, image)


def sum_over_gx(gram):
    size = lax.axis_size("gx")
    arrived = [
        lax.ppermute(gram, "gx", [(i, i ^ mask) for i in range(size)]) for mask in range(1, size)
    ]
    return sum(arrived, gram)


def all_parts(gram):
    gram = sum_over_gx(gram)
    return exchange(jnp.broadcast_to(gram, (lax.axis_size("gy"), *gram.shape)))


def exchange(blocks):
    return lax.all_to_all(blocks, "gy", split_axis=0, concat_axis=0, tiled=True)


def per_device(embeddings, start, requests, pairs, counts):
    rows_all = embeddings.shape[0] * lax.axis_size("gx") * lax.axis_size("gy")
    send_rows, rounded, table = prepare(embeddings, start, requests, pairs[0].T, counts)
    far_rows = exchange(send_rows)
    units, own, local_tiles, send_vecs, done = local_build(table, embeddings, rounded, requests.shape[1])
    far_vecs = exchange(send_vecs)
    wanted = far_rows[:, NOTE_BLOCK[0], NOTE_BLOCK[1]].astype(jnp.int32)
    back, start_gram, far_tiles = far_build(wanted, units, far_rows, rounded, done)
    returned = exchange(back)
    inverse = basis(rows_all, sum_over_gx(start_gram))
    own = far_first(wanted, far_tiles, far_vecs, own)
    rounded, first_gram, send_vecs = forward(table, own, returned, inverse)
    far_vecs = exchange(send_vecs)
    own, done = own_apply(local_tiles, rounded)
    returned = exchange(far_back(wanted, far_tiles, rounded, done))
    own = rest_apply(table, wanted, local_tiles, far_tiles, rounded, far_vecs, own)
    image, next_gram = assemble(table, own, returned)
    grams = all_parts(jnp.concatenate([first_gram, next_gram], axis=0))
    return last(rows_all, grams, image)


def solution(mesh):
    return jax.shard_map(
        per_device,
        mesh=mesh,
        in_specs=(
            P(("gx", "gy"), None),
            P(None, ("gx", "gy")),
            P(("gx", "gy"), None),
            P(("gx", "gy"), None, None),
            P(("gx", "gy")),
        ),
        out_specs=P(None, ("gx", "gy")),
        check_vma=False,
    )
```

```python
import functools

import jax
import jax.numpy as jnp
from jax import lax
from jax.experimental import pallas as pl
from jax.experimental.pallas import tpu as pltpu
from jax.sharding import PartitionSpec as P

D = 256
VECS = 32
BLK = 512
EXTRA = 9

FAR_ROW = 0
LOCAL = 32
LOCAL_COUNT = 96
FIRST_PEER = 128
NEXT_PEER = 160
TABLE = 192

NT = (((1,), (1,)), ((), ()))
NN = (((1,), (0,)), ((), ()))
SMEM = pl.BlockSpec(memory_space=pltpu.SMEM)
VMEM = pl.BlockSpec(memory_space=pltpu.VMEM)
HBM = pl.BlockSpec(memory_space=pltpu.HBM)
GROUP = 4
CHUNK = 2048
NOTE_ROWS = 16
PACK = 8
NOTE = BLK
NOTE_BLOCK = (NOTE + 8, D // 2)
LARGEST = 1e12
SENT = NOTE + NOTE_ROWS


def in_hbm(array):
    return pltpu.with_memory_space_constraint(array, pltpu.HBM)


def columns_of(block):
    return pl.ds(pl.multiple_of(block * BLK, BLK), BLK)


def params(limit_mib):
    return pltpu.CompilerParams(vmem_limit_bytes=limit_mib * 1024 * 1024)


def cost(flops, bytes_accessed):
    return pl.CostEstimate(flops=flops, bytes_accessed=bytes_accessed, transcendentals=0)


def three_parts(values):
    high = values.astype(jnp.bfloat16)
    rest = values - high.astype(jnp.float32)
    middle = rest.astype(jnp.bfloat16)
    low = (rest - middle.astype(jnp.float32)).astype(jnp.bfloat16)
    return high, middle, low


def factor_parts(factor):
    high, middle, low = three_parts(factor)
    return jnp.concatenate([high, high, high, middle, middle, low], axis=1)


def solved(factor, values):
    high, middle, low = three_parts(values)
    return dot_nn(factor, jnp.concatenate([high, middle, low, high, middle, high], axis=0))


def product(left, right):
    return solved(factor_parts(left), right)


def products(values):
    parts = jnp.concatenate(three_parts(values), axis=0)
    return dot_nt(parts, parts)


def sum_of_parts(total):
    total = total[:VECS] + total[VECS : 2 * VECS] + total[2 * VECS :]
    return total[:, :VECS] + total[:, VECS : 2 * VECS] + total[:, 2 * VECS :]


def packed(gram):
    return jnp.concatenate([gram[r : r + PACK] for r in range(0, VECS, PACK)], axis=1)


def unpacked(gram):
    return jnp.concatenate([gram[:, c : c + VECS] for c in range(0, gram.shape[1], VECS)], axis=0)


def normalized(rows):
    values = rows.astype(jnp.float32)
    scaled = values * lax.rsqrt(jnp.sum(values * values, axis=-1, keepdims=True) + 1e-06)
    return scaled.astype(jnp.bfloat16)


def note_slots(pairs, counts, table, block_count, peer_count):
    def clear(i, _):
        table[FAR_ROW + i] = -1
        table[FIRST_PEER + i] = -1
        return 0

    lax.fori_loop(0, peer_count, clear, 0)

    def note(k, local_count):
        row = pairs[0, k]
        col = pairs[1, k]
        far = col >= block_count
        crossed = jnp.logical_not(far) & (row != col)

        @pl.when(far)
        def _():
            peer = col - block_count
            table[FAR_ROW + peer] = row
            table[NEXT_PEER + peer] = table[FIRST_PEER + row]
            table[FIRST_PEER + row] = peer

        @pl.when(crossed)
        def _():
            table[LOCAL + local_count] = row * 64 + col

        return local_count + jnp.where(crossed, 1, 0)

    table[LOCAL_COUNT] = lax.fori_loop(0, counts[0], note, 0)


def each_peer_of(table, block, act):
    def one(peer):
        act(peer)
        return table[NEXT_PEER + peer]

    lax.while_loop(lambda peer: peer >= 0, one, table[FIRST_PEER + block])


def prepare_kernel(
    counts, all_pairs, all_requests, raw, start, send, rounded, table,
    pairs, requests, slot_sem, fresh, vecs, held, notes, load_sem, vec_sem, note_sem, send_sem,
):
    block_count = held.shape[0]
    peer_count = send.shape[0]

    def load(b):
        return pltpu.make_async_copy(raw.at[pl.ds(b * BLK, BLK), :], fresh.at[b], load_sem.at[b])

    def give(peer, b):
        return pltpu.make_async_copy(held.at[b], send.at[peer, pl.ds(0, NOTE), :], send_sem.at[peer])

    slot_loads = (
        pltpu.make_async_copy(all_pairs, pairs, slot_sem.at[0]),
        pltpu.make_async_copy(all_requests, requests, slot_sem.at[1]),
    )
    for slot_load in slot_loads:
        slot_load.start()
    vec_load = pltpu.make_async_copy(start, vecs, vec_sem)
    vec_load.start()
    for slot_load in slot_loads:
        slot_load.wait()
    note_slots(pairs, counts, table, block_count, peer_count)

    def begin(b, _):
        @pl.when(table[FIRST_PEER + b] >= 0)
        def _():
            load(b).start()

        return 0

    lax.fori_loop(0, block_count, begin, 0)

    vec_load.wait()
    gram = jnp.zeros((VECS, VECS), jnp.float32)
    for c in range(0, vecs.shape[1], CHUNK):
        w = vecs[:, c : c + CHUNK]
        rounded[:, c : c + CHUNK] = w.astype(jnp.bfloat16)
        w = jnp.clip(w, -LARGEST, LARGEST).astype(jnp.bfloat16)
        gram += dot_nt(w, w)
    high, middle, low = three_parts(packed(gram))

    def write_note(peer, _):
        block = jnp.full(low.shape, requests[0, peer].astype(jnp.float32), jnp.float32)
        notes[peer] = jnp.concatenate(
            [
                jnp.concatenate([high, middle], axis=1),
                jnp.concatenate([low, block.astype(jnp.bfloat16)], axis=1),
            ],
            axis=0,
        )
        return 0

    lax.fori_loop(0, peer_count, write_note, 0)
    note = pltpu.make_async_copy(notes, send.at[:, pl.ds(NOTE, NOTE_ROWS), :], note_sem)
    note.start()

    def one(b, _):
        @pl.when(table[FIRST_PEER + b] >= 0)
        def _():
            load(b).wait()
            held[b] = normalized(fresh[b])

            each_peer_of(table, b, lambda peer: give(peer, b).start())

        return 0

    lax.fori_loop(0, block_count, one, 0)

    def given(peer, _):
        row = table[FAR_ROW + peer]

        @pl.when(row >= 0)
        def _():
            give(peer, row).wait()

        return 0

    lax.fori_loop(0, peer_count, given, 0)
    note.wait()


def prepare(embeddings, start, requests, pairs, counts):
    peer_count = requests.shape[1]
    block_count = embeddings.shape[0] // BLK
    return pl.pallas_call(
        prepare_kernel,
        in_specs=[SMEM, HBM, HBM, HBM, HBM],
        out_specs=[HBM, VMEM, SMEM],
        out_shape=[
            pltpu.HBM((peer_count, SENT, D), jnp.bfloat16),
            jax.ShapeDtypeStruct(start.shape, jnp.bfloat16),
            jax.ShapeDtypeStruct((TABLE,), jnp.int32),
        ],
        scratch_shapes=[
            pltpu.SMEM(pairs.shape, jnp.int32),
            pltpu.SMEM(requests.shape, jnp.int32),
            pltpu.SemaphoreType.DMA((2,)),
            pltpu.VMEM((block_count, BLK, D), jnp.bfloat16),
            pltpu.VMEM(start.shape, jnp.float32),
            pltpu.VMEM((block_count, NOTE, D), jnp.bfloat16),
            pltpu.VMEM((peer_count, NOTE_ROWS, D), jnp.bfloat16),
            pltpu.SemaphoreType.DMA((block_count,)),
            pltpu.SemaphoreType.DMA,
            pltpu.SemaphoreType.DMA,
            pltpu.SemaphoreType.DMA((peer_count,)),
        ],
        compiler_params=params(20),
        cost_estimate=cost(10**7, 24 * 2**20),
        name="prepare",
    )(counts, in_hbm(pairs), in_hbm(requests), in_hbm(embeddings), in_hbm(start))


def tile_of(left, right):
    product = lax.dot_general(left, right, NT, preferred_element_type=jnp.float32)
    return (product * product * product).astype(jnp.bfloat16)


def dot_nt(vecs, tile):
    return lax.dot_general(vecs, tile, NT, preferred_element_type=jnp.float32)


def dot_nn(vecs, tile):
    return lax.dot_general(vecs, tile, NN, preferred_element_type=jnp.float32)


def local_build_kernel(
    table, raw, rounded, all_units, out, tiles, send, done,
    fresh, units, total, given, buffer, sem, unit_sem, keep_sem, save_sem, send_sem,
):
    block_count = units.shape[0]
    load = pltpu.make_async_copy(raw, fresh, unit_sem)
    load.start()
    count = block_count + table[LOCAL_COUNT]
    done[0] = count
    total[...] = jnp.zeros_like(total)
    spread(table, rounded, given)
    give = pltpu.make_async_copy(given, send, send_sem)
    give.start()
    load.wait()

    def normalize(b, _):
        units[b] = normalized(fresh[pl.ds(pl.multiple_of(b * BLK, BLK), BLK), :])
        return 0

    lax.fori_loop(0, block_count, normalize, 0)
    keep = pltpu.make_async_copy(units, all_units, keep_sem)
    keep.start()

    def copy(n):
        return pltpu.make_async_copy(buffer.at[n % 2], tiles.at[n], sem.at[n % 2])

    def one(n, _):
        code = table[LOCAL + jnp.maximum(n - block_count, 0)]
        row = jnp.where(n < block_count, n, code // 64)
        col = jnp.where(n < block_count, n, code % 64)

        @pl.when(n >= 2)
        def _():
            copy(n - 2).wait()

        tile = buffer.at[n % 2]
        tile[...] = tile_of(units[row], units[col])
        copy(n).start()
        total[:, columns_of(col)] += dot_nn(rounded[:, columns_of(row)], tile[...])

        @pl.when(row != col)
        def _():
            total[:, columns_of(row)] += dot_nt(rounded[:, columns_of(col)], tile[...])

        return 0

    lax.fori_loop(0, count, one, 0)

    @pl.when(count >= 2)
    def _():
        copy(count - 2).wait()

    @pl.when(count >= 1)
    def _():
        copy(count - 1).wait()

    save = pltpu.make_async_copy(total, out, save_sem)
    save.start()
    save.wait()
    keep.wait()
    give.wait()


def local_build(table, raw, rounded, peer_count):
    block_count = raw.shape[0] // BLK
    given = (peer_count, VECS, BLK)
    return pl.pallas_call(
        local_build_kernel,
        in_specs=[SMEM, HBM, VMEM],
        out_specs=[HBM, HBM, HBM, HBM, SMEM],
        out_shape=[
            pltpu.HBM((block_count, BLK, D), jnp.bfloat16),
            pltpu.HBM(rounded.shape, jnp.float32),
            pltpu.HBM((block_count + EXTRA, BLK, BLK), jnp.bfloat16),
            pltpu.HBM(given, jnp.bfloat16),
            jax.ShapeDtypeStruct((1,), jnp.int32),
        ],
        scratch_shapes=[
            pltpu.VMEM(raw.shape, jnp.bfloat16),
            pltpu.VMEM((block_count, BLK, D), jnp.bfloat16),
            pltpu.VMEM(rounded.shape, jnp.float32),
            pltpu.VMEM(given, jnp.bfloat16),
            pltpu.VMEM((2, BLK, BLK), jnp.bfloat16),
            pltpu.SemaphoreType.DMA((2,)),
            pltpu.SemaphoreType.DMA,
            pltpu.SemaphoreType.DMA,
            pltpu.SemaphoreType.DMA,
            pltpu.SemaphoreType.DMA,
        ],
        compiler_params=params(20),
        cost_estimate=cost(33 * 2 * BLK * BLK * (D + 8 * VECS), 32 * 2**20),
        name="local_build",
    )(table, in_hbm(raw), rounded)


def spread(table, source, out):
    def give(peer, _):
        row = table[FAR_ROW + peer]

        @pl.when(row >= 0)
        def _():
            out[peer] = source[:, columns_of(row)]

        return 0

    lax.fori_loop(0, out.shape[0], give, 0)


def note_active(wanted, active):
    def one(peer, count):
        @pl.when(wanted[peer] >= 0)
        def _():
            active[count] = peer

        return count + jnp.where(wanted[peer] >= 0, 1, 0)

    return lax.fori_loop(0, wanted.shape[0], one, 0)


def tile_loads(wanted, active, units, far_rows, near, far, load_sem, n):
    peer = active[n]
    return (
        pltpu.make_async_copy(far_rows.at[peer, pl.ds(0, BLK), :], far.at[n], load_sem.at[0, n]),
        pltpu.make_async_copy(units.at[wanted[peer]], near.at[n], load_sem.at[1, n]),
    )


def far_build_kernel(
    wanted, units, far_rows, rounded, after, back, gram, tiles,
    active, near, far, buffer, load_sem, save_sem, notes, note_sem,
):
    del after
    note_load = pltpu.make_async_copy(far_rows.at[:, pl.ds(NOTE, NOTE_ROWS), :], notes, note_sem)
    count = note_active(wanted, active)
    loads = functools.partial(tile_loads, wanted, active, units, far_rows, near, far, load_sem)

    def save(n, z):
        return pltpu.make_async_copy(buffer.at[z], tiles.at[active[n]], save_sem.at[z])

    def begin(n, _):
        for load in loads(n):
            load.start()
        return 0

    def group(first, base):
        for z in range(GROUP):

            @pl.when(first + z < count)
            def _(n=first + z):
                for load in loads(n):
                    load.wait()

        @pl.when(first >= 2 * GROUP)
        def _():
            for z in range(GROUP):
                save(first - 2 * GROUP + z, base + z).wait()

        held = [jnp.minimum(first + z, count - 1) for z in range(GROUP)]
        peers = [active[n] for n in held]
        for z, n in enumerate(held):
            buffer[base + z] = tile_of(near[n], far[n])
        for z, peer in enumerate(peers):
            vecs = rounded[:, columns_of(wanted[peer])]
            back[peer] = dot_nn(vecs, buffer[base + z]).astype(jnp.bfloat16)
        for z in range(GROUP):

            @pl.when(first + z < count)
            def _(n=first + z, z=z):
                save(n, base + z).start()

    def two_groups(i, _):
        first = 2 * GROUP * i
        group(first, 0)

        @pl.when(first + GROUP < count)
        def _():
            group(first + GROUP, GROUP)

        return 0

    lax.fori_loop(0, count, begin, 0)
    note_load.start()
    lax.fori_loop(0, (count + 2 * GROUP - 1) // (2 * GROUP), two_groups, 0)
    note_load.wait()
    total = jnp.sum(notes[...].astype(jnp.float32), axis=0)
    half = D // 2
    gram[...] = total[:PACK, :half] + total[:PACK, half:] + total[PACK:, :half]
    for z in range(2 * GROUP):
        newest = z + 2 * GROUP * ((count - 1 - z) // (2 * GROUP))

        @pl.when((count > z) & (newest // GROUP * GROUP + 2 * GROUP >= count))
        def _(n=newest, z=z):
            save(n, z).wait()


def far_build(wanted, units, far_rows, rounded, after):
    peer_count = far_rows.shape[0]
    return pl.pallas_call(
        far_build_kernel,
        in_specs=[SMEM, HBM, HBM, VMEM, SMEM],
        out_specs=[VMEM, VMEM, HBM],
        out_shape=[
            jax.ShapeDtypeStruct((peer_count, VECS, BLK), jnp.bfloat16),
            jax.ShapeDtypeStruct((PACK, VECS * VECS // PACK), jnp.float32),
            pltpu.HBM((peer_count, BLK, BLK), jnp.bfloat16),
        ],
        scratch_shapes=[
            pltpu.SMEM((peer_count,), jnp.int32),
            pltpu.VMEM((peer_count, BLK, D), jnp.bfloat16),
            pltpu.VMEM((peer_count, BLK, D), jnp.bfloat16),
            pltpu.VMEM((2 * GROUP, BLK, BLK), jnp.bfloat16),
            pltpu.SemaphoreType.DMA((2, peer_count)),
            pltpu.SemaphoreType.DMA((2 * GROUP,)),
            pltpu.VMEM((peer_count, NOTE_ROWS, D), jnp.bfloat16),
            pltpu.SemaphoreType.DMA,
        ],
        compiler_params=params(28),
        cost_estimate=cost(32 * 2 * BLK * BLK * (D + 4 * VECS), 34 * 2**20),
        name="far_build",
    )(wanted, in_hbm(units), in_hbm(far_rows), rounded, after)


def stream(count, source_of, buffer, sem, base=0):
    def load(n):
        return pltpu.make_async_copy(source_of(n), buffer.at[base + n], sem.at[base + n])

    def begin(n, _):
        load(n).start()
        return 0

    lax.fori_loop(0, count, begin, 0)

    def work(use):
        def group(g, _):
            first = g * GROUP
            for z in range(GROUP):

                @pl.when(first + z < count)
                def _(n=first + z):
                    load(n).wait()

            held = [jnp.minimum(first + z, count - 1) for z in range(GROUP)]
            live = [first + z < count for z in range(GROUP)]
            use(held, live, [buffer.at[base + n] for n in held])
            return 0

        lax.fori_loop(0, (count + GROUP - 1) // GROUP, group, 0)

    return work


def tile_scratch(tiles):
    return [
        pltpu.VMEM((tiles, BLK, BLK), jnp.bfloat16),
        pltpu.SemaphoreType.DMA((tiles,)),
    ]


def masked(live, vecs):
    return jnp.where(live, vecs, jnp.zeros_like(vecs))


def own_apply_kernel(tiles, rounded, out, done, total, buffer, sem, save_sem):
    count = rounded.shape[1] // BLK
    done[0] = count
    work = stream(count, lambda n: tiles.at[n], buffer, sem)

    def use(held, live, group):
        terms = [dot_nn(rounded[:, columns_of(n)], tile[...]) for n, tile in zip(held, group)]
        for n, term in zip(held, terms):
            total[:, columns_of(n)] = term

    work(use)
    save = pltpu.make_async_copy(total, out, save_sem)
    save.start()
    save.wait()


def own_apply(tiles, rounded):
    return pl.pallas_call(
        own_apply_kernel,
        in_specs=[HBM, VMEM],
        out_specs=[HBM, SMEM],
        out_shape=[
            pltpu.HBM(rounded.shape, jnp.float32),
            jax.ShapeDtypeStruct((1,), jnp.int32),
        ],
        scratch_shapes=[
            pltpu.VMEM(rounded.shape, jnp.float32),
            *tile_scratch(rounded.shape[1] // BLK),
            pltpu.SemaphoreType.DMA,
        ],
        compiler_params=params(20),
        cost_estimate=cost(24 * 2 * BLK * BLK * 4 * VECS, 13 * 2**20),
        name="own_apply",
    )(in_hbm(tiles), rounded)


def far_back_kernel(wanted, tiles, rounded, after, back, active, buffer, sem):
    del after
    count = note_active(wanted, active)
    work = stream(count, lambda n: tiles.at[active[n]], buffer, sem)

    def use(held, live, group):
        peers = [active[n] for n in held]
        terms = [
            dot_nn(rounded[:, columns_of(wanted[peer])], tile[...]) for peer, tile in zip(peers, group)
        ]
        for peer, term in zip(peers, terms):
            back[peer] = term.astype(jnp.bfloat16)

    work(use)


def far_back(wanted, tiles, rounded, after):
    peer_count = tiles.shape[0]
    return pl.pallas_call(
        far_back_kernel,
        in_specs=[SMEM, HBM, VMEM, SMEM],
        out_specs=VMEM,
        out_shape=jax.ShapeDtypeStruct((peer_count, VECS, BLK), jnp.bfloat16),
        scratch_shapes=[pltpu.SMEM((peer_count,), jnp.int32), *tile_scratch(peer_count)],
        compiler_params=params(24),
        cost_estimate=cost(32 * 2 * BLK * BLK * 4 * VECS, 17 * 2**20),
        name="far_back",
    )(wanted, in_hbm(tiles), rounded, after)


def add_far(wanted, far_vecs, total, active, work):
    def use(held, live, group):
        peers = [active[n] for n in held]
        terms = [
            dot_nt(masked(alive, far_vecs[peer]), tile[...])
            for peer, alive, tile in zip(peers, live, group)
        ]
        for peer, term in zip(peers, terms):
            total[:, columns_of(wanted[peer])] += term

    work(use)


def far_first_kernel(wanted, tiles, far_vecs, before, total, active, buffer, sem, before_sem):
    before_load = pltpu.make_async_copy(before, total, before_sem)
    before_load.start()
    count = note_active(wanted, active)
    work = stream(count, lambda n: tiles.at[active[n]], buffer, sem)
    before_load.wait()
    add_far(wanted, far_vecs, total, active, work)


def far_first(wanted, tiles, far_vecs, before):
    return pl.pallas_call(
        far_first_kernel,
        in_specs=[SMEM, HBM, VMEM, HBM],
        out_specs=VMEM,
        out_shape=jax.ShapeDtypeStruct(before.shape, jnp.float32),
        scratch_shapes=[
            pltpu.SMEM(wanted.shape, jnp.int32),
            *tile_scratch(wanted.shape[0]),
            pltpu.SemaphoreType.DMA,
        ],
        compiler_params=params(28),
        cost_estimate=cost(32 * 2 * BLK * BLK * 4 * VECS, 20 * 2**20),
        name="far_first",
    )(wanted, in_hbm(tiles), far_vecs, in_hbm(before))


def rest_apply_kernel(
    table, wanted, local_tiles, far_tiles, rounded, far_vecs, before, total, active, buffer, sem, before_sem
):
    block_count = rounded.shape[1] // BLK
    before_load = pltpu.make_async_copy(before, total, before_sem)
    before_load.start()
    crossed_work = stream(table[LOCAL_COUNT], lambda n: local_tiles.at[block_count + n], buffer, sem)
    count = note_active(wanted, active)
    far_work = stream(count, lambda n: far_tiles.at[active[n]], buffer, sem, EXTRA)
    before_load.wait()

    def use_crossed(held, live, group):
        codes = [table[LOCAL + n] for n in held]
        pairs = [(code // 64, code % 64) for code in codes]
        vecs = [[masked(alive, rounded[:, columns_of(b)]) for b in pair] for pair, alive in zip(pairs, live)]
        to_col = [dot_nn(row_vecs, tile[...]) for (row_vecs, _), tile in zip(vecs, group)]
        to_row = [dot_nt(col_vecs, tile[...]) for (_, col_vecs), tile in zip(vecs, group)]
        for (row, col), row_term, col_term in zip(pairs, to_row, to_col):
            total[:, columns_of(col)] += col_term
            total[:, columns_of(row)] += row_term

    crossed_work(use_crossed)
    add_far(wanted, far_vecs, total, active, far_work)


def rest_apply(table, wanted, local_tiles, far_tiles, rounded, far_vecs, before):
    return pl.pallas_call(
        rest_apply_kernel,
        in_specs=[SMEM, SMEM, HBM, HBM, VMEM, VMEM, HBM],
        out_specs=VMEM,
        out_shape=jax.ShapeDtypeStruct(before.shape, jnp.float32),
        scratch_shapes=[
            pltpu.SMEM(wanted.shape, jnp.int32),
            *tile_scratch(EXTRA + wanted.shape[0]),
            pltpu.SemaphoreType.DMA,
        ],
        compiler_params=params(30),
        cost_estimate=cost(40 * 2 * BLK * BLK * 4 * VECS, 24 * 2**20),
        name="rest_apply",
    )(table, wanted, in_hbm(local_tiles), in_hbm(far_tiles), rounded, far_vecs, in_hbm(before))


def add_returned(table, own, returned, image):
    image[...] = own[...]

    def add(peer, _):
        row = table[FAR_ROW + peer]

        @pl.when(row >= 0)
        def _():
            image[:, columns_of(row)] += returned[peer].astype(jnp.float32)

        return 0

    lax.fori_loop(0, returned.shape[0], add, 0)


def gram_kernel(image, gram):
    total = jnp.zeros((3 * VECS, 3 * VECS), jnp.float32)
    for c in range(0, image.shape[1], CHUNK):
        total += products(image[:, c : c + CHUNK])
    gram[...] = packed(sum_of_parts(total))


def forward_kernel(table, own, returned, inverse, rounded, gram, send, image, sem):
    factor = factor_parts(inverse[...])
    add_returned(table, own, returned, image)

    def copy(peer, row):
        return pltpu.make_async_copy(rounded.at[:, columns_of(row)], send.at[peer], sem.at[peer])

    for c in range(0, image.shape[1], CHUNK):
        based = solved(factor, image[:, c : c + CHUNK])
        image[:, c : c + CHUNK] = based
        rounded[:, c : c + CHUNK] = based.astype(jnp.bfloat16)
        for block in range(c // BLK, (c + CHUNK) // BLK):
            each_peer_of(table, block, lambda peer, block=block: copy(peer, block).start())
    gram_kernel(image, gram)

    def finish(peer, _):
        row = table[FAR_ROW + peer]

        @pl.when(row >= 0)
        def _():
            copy(peer, row).wait()

        return 0

    lax.fori_loop(0, send.shape[0], finish, 0)


def forward(table, own, returned, inverse):
    return pl.pallas_call(
        forward_kernel,
        in_specs=[SMEM, VMEM, VMEM, VMEM],
        out_specs=[VMEM, VMEM, HBM],
        out_shape=[
            jax.ShapeDtypeStruct(own.shape, jnp.bfloat16),
            jax.ShapeDtypeStruct((PACK, VECS * VECS // PACK), jnp.float32),
            pltpu.HBM(returned.shape, jnp.bfloat16),
        ],
        scratch_shapes=[
            pltpu.VMEM(own.shape, jnp.float32),
            pltpu.SemaphoreType.DMA((returned.shape[0],)),
        ],
        compiler_params=params(12),
        cost_estimate=cost(10**8, 5 * 2**20),
        name="forward",
    )(table, own, returned, inverse)


def assemble_kernel(table, own, returned, image, gram):
    add_returned(table, own, returned, image)
    gram_kernel(image, gram)


def assemble(table, own, returned):
    return pl.pallas_call(
        assemble_kernel,
        in_specs=[SMEM, VMEM, VMEM],
        out_specs=[VMEM, VMEM],
        out_shape=[
            jax.ShapeDtypeStruct(own.shape, jnp.float32),
            jax.ShapeDtypeStruct((PACK, VECS * VECS // PACK), jnp.float32),
        ],
        compiler_params=params(10),
        cost_estimate=cost(10**8, 5 * 2**20),
        name="assemble",
    )(table, own, returned)


def inverse_factor(matrix):
    both = (VECS, 2 * VECS)
    rows = lax.broadcasted_iota(jnp.int32, both, 0)
    lanes = lax.broadcasted_iota(jnp.int32, both, 1)
    work = jnp.where(
        lanes < VECS,
        jnp.concatenate([matrix, matrix], axis=1),
        jnp.where(rows + VECS == lanes, 1.0, 0.0),
    )
    for k in range(0, VECS, 2):
        first_col = jnp.broadcast_to(work[:, k : k + 1], both)
        next_col = jnp.broadcast_to(work[:, k + 1 : k + 2], both)
        scale = lax.rsqrt(first_col[k : k + 1])
        first_row = work[k : k + 1] * scale
        cross = next_col[k : k + 1] * scale
        next_scale = lax.rsqrt(next_col[k + 1 : k + 2] - cross * cross)
        next_row = (work[k + 1 : k + 2] - cross * first_row) * next_scale
        first_factor = first_col * scale
        next_factor = (next_col - first_factor * cross) * next_scale
        rest = work - (first_factor * first_row + next_factor * next_row)
        kept = jnp.where(rows == k, first_row, jnp.where(rows == k + 1, next_row, work))
        work = jnp.where(rows > k + 1, rest, kept)
    return work[:, VECS:]


def identity():
    rows = lax.broadcasted_iota(jnp.int32, (VECS, VECS), 0)
    lanes = lax.broadcasted_iota(jnp.int32, (VECS, VECS), 1)
    return jnp.where(rows == lanes, 1.0, 0.0).astype(jnp.float32)


def basis_kernel(rows_all, gram, inverse):
    eye = identity()
    matrix = unpacked(gram[...]) * (1.0 / rows_all)
    factor = inverse_factor(matrix * (1.0 + 1e-3 * eye))
    usable = jnp.sum(jnp.abs(factor)) < 1e30
    inverse[...] = jnp.where(usable, factor, eye)


def basis(rows_all, gram):
    return pl.pallas_call(
        functools.partial(basis_kernel, rows_all),
        in_specs=[VMEM],
        out_specs=VMEM,
        out_shape=jax.ShapeDtypeStruct((VECS, VECS), jnp.float32),
        compiler_params=params(4),
        cost_estimate=cost(10**6, 10**4),
        name="basis",
    )(gram)


def last_kernel(rows_all, grams, image, out, vectors, sem):
    both = jnp.sum(grams[...], axis=0) * (1.0 / rows_all)
    first = inverse_factor(unpacked(both[:PACK]))
    high, middle, low = three_parts(first)
    turned = dot_nt(
        factor_parts(product(first, unpacked(both[PACK:]))),
        jnp.concatenate([high, middle, low, high, middle, high], axis=1),
    )
    factor = factor_parts(product(inverse_factor(turned), first))
    copies = []
    for c in range(0, image.shape[1], CHUNK):
        columns = pl.ds(c, CHUNK)
        vectors[:, columns] = solved(factor, image[:, columns])
        copies.append(pltpu.make_async_copy(vectors.at[:, columns], out.at[:, columns], sem.at[c // CHUNK]))
        copies[-1].start()
    for copy in copies:
        copy.wait()


def last(rows_all, grams, image):
    return pl.pallas_call(
        functools.partial(last_kernel, rows_all),
        in_specs=[VMEM, VMEM],
        out_specs=HBM,
        out_shape=jax.ShapeDtypeStruct(image.shape, jnp.float32),
        scratch_shapes=[
            pltpu.VMEM(image.shape, jnp.float32),
            pltpu.SemaphoreType.DMA((image.shape[1] // CHUNK,)),
        ],
        compiler_params=params(10),
        cost_estimate=cost(10**8, 4 * 2**20),
        name="last",
    )(grams, image)


def sum_over_gx(gram):
    size = lax.axis_size("gx")
    arrived = [
        lax.ppermute(gram, "gx", [(i, i ^ mask) for i in range(size)]) for mask in range(1, size)
    ]
    return sum(arrived, gram)


def all_parts(gram):
    gram = sum_over_gx(gram)
    return exchange(jnp.broadcast_to(gram, (lax.axis_size("gy"), *gram.shape)))


def exchange(blocks):
    return lax.all_to_all(blocks, "gy", split_axis=0, concat_axis=0, tiled=True)


def per_device(embeddings, start, requests, pairs, counts):
    rows_all = embeddings.shape[0] * lax.axis_size("gx") * lax.axis_size("gy")
    send_rows, rounded, table = prepare(embeddings, start, requests, pairs[0].T, counts)
    far_rows = exchange(send_rows)
    units, own, local_tiles, send_vecs, done = local_build(table, embeddings, rounded, requests.shape[1])
    far_vecs = exchange(send_vecs)
    wanted = far_rows[:, NOTE_BLOCK[0], NOTE_BLOCK[1]].astype(jnp.int32)
    back, start_gram, far_tiles = far_build(wanted, units, far_rows, rounded, done)
    returned = exchange(back)
    inverse = basis(rows_all, sum_over_gx(start_gram))
    own = far_first(wanted, far_tiles, far_vecs, own)
    rounded, first_gram, send_vecs = forward(table, own, returned, inverse)
    far_vecs = exchange(send_vecs)
    own, done = own_apply(local_tiles, rounded)
    returned = exchange(far_back(wanted, far_tiles, rounded, done))
    own = rest_apply(table, wanted, local_tiles, far_tiles, rounded, far_vecs, own)
    image, next_gram = assemble(table, own, returned)
    grams = all_parts(jnp.concatenate([first_gram, next_gram], axis=0))
    return last(rows_all, grams, image)


def solution(mesh):
    return jax.shard_map(
        per_device,
        mesh=mesh,
        in_specs=(
            P(("gx", "gy"), None),
            P(None, ("gx", "gy")),
            P(("gx", "gy"), None),
            P(("gx", "gy"), None, None),
            P(("gx", "gy")),
        ),
        out_specs=P(None, ("gx", "gy")),
        check_vma=False,
    )
```

```python
import functools

import jax
import jax.numpy as jnp
from jax import lax
from jax.experimental import pallas as pl
from jax.experimental.pallas import tpu as pltpu
from jax.sharding import PartitionSpec as P

D = 256
VECS = 32
BLK = 512
EXTRA = 9
LATE = 8

FAR_ROW = 0
LOCAL = 32
LOCAL_COUNT = 96
FIRST_PEER = 128
NEXT_PEER = 160
TABLE = 192

NT = (((1,), (1,)), ((), ()))
NN = (((1,), (0,)), ((), ()))
SMEM = pl.BlockSpec(memory_space=pltpu.SMEM)
VMEM = pl.BlockSpec(memory_space=pltpu.VMEM)
HBM = pl.BlockSpec(memory_space=pltpu.HBM)
GROUP = 4
CHUNK = 2048
NOTE_ROWS = 16
PACK = 8
NOTE = BLK
NOTE_BLOCK = (NOTE + 8, D // 2)
LARGEST = 1e12
SENT = NOTE + NOTE_ROWS


def in_hbm(array):
    return pltpu.with_memory_space_constraint(array, pltpu.HBM)


def columns_of(block):
    return pl.ds(pl.multiple_of(block * BLK, BLK), BLK)


def params(limit_mib):
    return pltpu.CompilerParams(vmem_limit_bytes=limit_mib * 1024 * 1024)


def cost(flops, bytes_accessed):
    return pl.CostEstimate(flops=flops, bytes_accessed=bytes_accessed, transcendentals=0)


def three_parts(values):
    high = values.astype(jnp.bfloat16)
    rest = values - high.astype(jnp.float32)
    middle = rest.astype(jnp.bfloat16)
    low = (rest - middle.astype(jnp.float32)).astype(jnp.bfloat16)
    return high, middle, low


def factor_parts(factor):
    high, middle, low = three_parts(factor)
    return jnp.concatenate([high, high, high, middle, middle, low], axis=1)


def solved(factor, values):
    high, middle, low = three_parts(values)
    return dot_nn(factor, jnp.concatenate([high, middle, low, high, middle, high], axis=0))


def product(left, right):
    return solved(factor_parts(left), right)


def products(values):
    parts = jnp.concatenate(three_parts(values), axis=0)
    return dot_nt(parts, parts)


def sum_of_parts(total):
    total = total[:VECS] + total[VECS : 2 * VECS] + total[2 * VECS :]
    return total[:, :VECS] + total[:, VECS : 2 * VECS] + total[:, 2 * VECS :]


def packed(gram):
    return jnp.concatenate([gram[r : r + PACK] for r in range(0, VECS, PACK)], axis=1)


def unpacked(gram):
    return jnp.concatenate([gram[:, c : c + VECS] for c in range(0, gram.shape[1], VECS)], axis=0)


def normalized(rows):
    values = rows.astype(jnp.float32)
    scaled = values * lax.rsqrt(jnp.sum(values * values, axis=-1, keepdims=True) + 1e-06)
    return scaled.astype(jnp.bfloat16)


def note_slots(pairs, counts, table, block_count, peer_count):
    def clear(i, _):
        table[FAR_ROW + i] = -1
        table[FIRST_PEER + i] = -1
        return 0

    lax.fori_loop(0, peer_count, clear, 0)

    def note(k, local_count):
        row = pairs[0, k]
        col = pairs[1, k]
        far = col >= block_count
        crossed = jnp.logical_not(far) & (row != col)

        @pl.when(far)
        def _():
            peer = col - block_count
            table[FAR_ROW + peer] = row
            table[NEXT_PEER + peer] = table[FIRST_PEER + row]
            table[FIRST_PEER + row] = peer

        @pl.when(crossed)
        def _():
            table[LOCAL + local_count] = row * 64 + col

        return local_count + jnp.where(crossed, 1, 0)

    table[LOCAL_COUNT] = lax.fori_loop(0, counts[0], note, 0)


def each_peer_of(table, block, act):
    def one(peer):
        act(peer)
        return table[NEXT_PEER + peer]

    lax.while_loop(lambda peer: peer >= 0, one, table[FIRST_PEER + block])


def prepare_kernel(
    counts, all_pairs, all_requests, raw, start, send, rounded, table,
    pairs, requests, slot_sem, fresh, vecs, held, notes, load_sem, vec_sem, note_sem, send_sem,
):
    block_count = held.shape[0]
    peer_count = send.shape[0]

    def load(b):
        return pltpu.make_async_copy(raw.at[pl.ds(b * BLK, BLK), :], fresh.at[b], load_sem.at[b])

    def give(peer, b):
        return pltpu.make_async_copy(held.at[b], send.at[peer, pl.ds(0, NOTE), :], send_sem.at[peer])

    slot_loads = (
        pltpu.make_async_copy(all_pairs, pairs, slot_sem.at[0]),
        pltpu.make_async_copy(all_requests, requests, slot_sem.at[1]),
    )
    for slot_load in slot_loads:
        slot_load.start()
    vec_load = pltpu.make_async_copy(start, vecs, vec_sem)
    vec_load.start()
    for slot_load in slot_loads:
        slot_load.wait()
    note_slots(pairs, counts, table, block_count, peer_count)

    def begin(b, _):
        @pl.when(table[FIRST_PEER + b] >= 0)
        def _():
            load(b).start()

        return 0

    lax.fori_loop(0, block_count, begin, 0)

    vec_load.wait()
    gram = jnp.zeros((VECS, VECS), jnp.float32)
    for c in range(0, vecs.shape[1], CHUNK):
        w = vecs[:, c : c + CHUNK]
        rounded[:, c : c + CHUNK] = w.astype(jnp.bfloat16)
        w = jnp.clip(w, -LARGEST, LARGEST).astype(jnp.bfloat16)
        gram += dot_nt(w, w)
    high, middle, low = three_parts(packed(gram))

    def write_note(peer, _):
        block = jnp.full(low.shape, requests[0, peer].astype(jnp.float32), jnp.float32)
        notes[peer] = jnp.concatenate(
            [
                jnp.concatenate([high, middle], axis=1),
                jnp.concatenate([low, block.astype(jnp.bfloat16)], axis=1),
            ],
            axis=0,
        )
        return 0

    lax.fori_loop(0, peer_count, write_note, 0)
    note = pltpu.make_async_copy(notes, send.at[:, pl.ds(NOTE, NOTE_ROWS), :], note_sem)
    note.start()

    def one(b, _):
        @pl.when(table[FIRST_PEER + b] >= 0)
        def _():
            load(b).wait()
            held[b] = normalized(fresh[b])

            each_peer_of(table, b, lambda peer: give(peer, b).start())

        return 0

    lax.fori_loop(0, block_count, one, 0)

    def given(peer, _):
        row = table[FAR_ROW + peer]

        @pl.when(row >= 0)
        def _():
            give(peer, row).wait()

        return 0

    lax.fori_loop(0, peer_count, given, 0)
    note.wait()


def prepare(embeddings, start, requests, pairs, counts):
    peer_count = requests.shape[1]
    block_count = embeddings.shape[0] // BLK
    return pl.pallas_call(
        prepare_kernel,
        in_specs=[SMEM, HBM, HBM, HBM, HBM],
        out_specs=[HBM, VMEM, SMEM],
        out_shape=[
            pltpu.HBM((peer_count, SENT, D), jnp.bfloat16),
            jax.ShapeDtypeStruct(start.shape, jnp.bfloat16),
            jax.ShapeDtypeStruct((TABLE,), jnp.int32),
        ],
        scratch_shapes=[
            pltpu.SMEM(pairs.shape, jnp.int32),
            pltpu.SMEM(requests.shape, jnp.int32),
            pltpu.SemaphoreType.DMA((2,)),
            pltpu.VMEM((block_count, BLK, D), jnp.bfloat16),
            pltpu.VMEM(start.shape, jnp.float32),
            pltpu.VMEM((block_count, NOTE, D), jnp.bfloat16),
            pltpu.VMEM((peer_count, NOTE_ROWS, D), jnp.bfloat16),
            pltpu.SemaphoreType.DMA((block_count,)),
            pltpu.SemaphoreType.DMA,
            pltpu.SemaphoreType.DMA,
            pltpu.SemaphoreType.DMA((peer_count,)),
        ],
        compiler_params=params(20),
        cost_estimate=cost(10**7, 24 * 2**20),
        name="prepare",
    )(counts, in_hbm(pairs), in_hbm(requests), in_hbm(embeddings), in_hbm(start))


def tile_of(left, right):
    product = lax.dot_general(left, right, NT, preferred_element_type=jnp.float32)
    return (product * product * product).astype(jnp.bfloat16)


def dot_nt(vecs, tile):
    return lax.dot_general(vecs, tile, NT, preferred_element_type=jnp.float32)


def dot_nn(vecs, tile):
    return lax.dot_general(vecs, tile, NN, preferred_element_type=jnp.float32)


def local_build_kernel(
    table, raw, rounded, all_units, out, tiles, send, done,
    fresh, units, total, given, buffer, sem, unit_sem, keep_sem, save_sem, send_sem,
):
    block_count = units.shape[0]
    load = pltpu.make_async_copy(raw, fresh, unit_sem)
    load.start()
    count = block_count + table[LOCAL_COUNT]
    done[0] = count
    total[...] = jnp.zeros_like(total)
    spread(table, rounded, given)
    give = pltpu.make_async_copy(given, send, send_sem)
    give.start()
    load.wait()

    def normalize(b, _):
        units[b] = normalized(fresh[pl.ds(pl.multiple_of(b * BLK, BLK), BLK), :])
        return 0

    lax.fori_loop(0, block_count, normalize, 0)
    keep = pltpu.make_async_copy(units, all_units, keep_sem)
    keep.start()

    def copy(n):
        return pltpu.make_async_copy(buffer.at[n % 2], tiles.at[n], sem.at[n % 2])

    def one(n, _):
        code = table[LOCAL + jnp.maximum(n - block_count, 0)]
        row = jnp.where(n < block_count, n, code // 64)
        col = jnp.where(n < block_count, n, code % 64)

        @pl.when(n >= 2)
        def _():
            copy(n - 2).wait()

        tile = buffer.at[n % 2]
        tile[...] = tile_of(units[row], units[col])
        copy(n).start()
        total[:, columns_of(col)] += dot_nn(rounded[:, columns_of(row)], tile[...])

        @pl.when(row != col)
        def _():
            total[:, columns_of(row)] += dot_nt(rounded[:, columns_of(col)], tile[...])

        return 0

    lax.fori_loop(0, count, one, 0)

    @pl.when(count >= 2)
    def _():
        copy(count - 2).wait()

    @pl.when(count >= 1)
    def _():
        copy(count - 1).wait()

    save = pltpu.make_async_copy(total, out, save_sem)
    save.start()
    save.wait()
    keep.wait()
    give.wait()


def local_build(table, raw, rounded, peer_count):
    block_count = raw.shape[0] // BLK
    given = (peer_count, VECS, BLK)
    return pl.pallas_call(
        local_build_kernel,
        in_specs=[SMEM, HBM, VMEM],
        out_specs=[HBM, HBM, HBM, HBM, SMEM],
        out_shape=[
            pltpu.HBM((block_count, BLK, D), jnp.bfloat16),
            pltpu.HBM(rounded.shape, jnp.float32),
            pltpu.HBM((block_count + EXTRA, BLK, BLK), jnp.bfloat16),
            pltpu.HBM(given, jnp.bfloat16),
            jax.ShapeDtypeStruct((1,), jnp.int32),
        ],
        scratch_shapes=[
            pltpu.VMEM(raw.shape, jnp.bfloat16),
            pltpu.VMEM((block_count, BLK, D), jnp.bfloat16),
            pltpu.VMEM(rounded.shape, jnp.float32),
            pltpu.VMEM(given, jnp.bfloat16),
            pltpu.VMEM((2, BLK, BLK), jnp.bfloat16),
            pltpu.SemaphoreType.DMA((2,)),
            pltpu.SemaphoreType.DMA,
            pltpu.SemaphoreType.DMA,
            pltpu.SemaphoreType.DMA,
            pltpu.SemaphoreType.DMA,
        ],
        compiler_params=params(20),
        cost_estimate=cost(33 * 2 * BLK * BLK * (D + 8 * VECS), 32 * 2**20),
        name="local_build",
    )(table, in_hbm(raw), rounded)


def spread(table, source, out):
    def give(peer, _):
        row = table[FAR_ROW + peer]

        @pl.when(row >= 0)
        def _():
            out[peer] = source[:, columns_of(row)]

        return 0

    lax.fori_loop(0, out.shape[0], give, 0)


def note_active(wanted, active):
    def one(peer, count):
        @pl.when(wanted[peer] >= 0)
        def _():
            active[count] = peer

        return count + jnp.where(wanted[peer] >= 0, 1, 0)

    return lax.fori_loop(0, wanted.shape[0], one, 0)


def tile_loads(wanted, active, units, far_rows, near, far, load_sem, n):
    peer = active[n]
    return (
        pltpu.make_async_copy(far_rows.at[peer, pl.ds(0, BLK), :], far.at[n], load_sem.at[0, n]),
        pltpu.make_async_copy(units.at[wanted[peer]], near.at[n], load_sem.at[1, n]),
    )


def far_build_kernel(
    wanted, units, far_rows, rounded, after, back, gram, tiles,
    active, near, far, buffer, load_sem, save_sem, notes, note_sem,
):
    del after
    note_load = pltpu.make_async_copy(far_rows.at[:, pl.ds(NOTE, NOTE_ROWS), :], notes, note_sem)
    count = note_active(wanted, active)
    loads = functools.partial(tile_loads, wanted, active, units, far_rows, near, far, load_sem)

    def save(n, z):
        return pltpu.make_async_copy(buffer.at[z], tiles.at[active[n]], save_sem.at[z])

    def begin(n, _):
        for load in loads(n):
            load.start()
        return 0

    def group(first, base):
        for z in range(GROUP):

            @pl.when(first + z < count)
            def _(n=first + z):
                for load in loads(n):
                    load.wait()

        @pl.when(first >= 2 * GROUP)
        def _():
            for z in range(GROUP):
                save(first - 2 * GROUP + z, base + z).wait()

        held = [jnp.minimum(first + z, count - 1) for z in range(GROUP)]
        peers = [active[n] for n in held]
        for z, n in enumerate(held):
            buffer[base + z] = tile_of(near[n], far[n])
        for z, peer in enumerate(peers):
            vecs = rounded[:, columns_of(wanted[peer])]
            back[peer] = dot_nn(vecs, buffer[base + z]).astype(jnp.bfloat16)
        for z in range(GROUP):

            @pl.when(first + z < count)
            def _(n=first + z, z=z):
                save(n, base + z).start()

    def two_groups(i, _):
        first = 2 * GROUP * i
        group(first, 0)

        @pl.when(first + GROUP < count)
        def _():
            group(first + GROUP, GROUP)

        return 0

    lax.fori_loop(0, count, begin, 0)
    note_load.start()
    lax.fori_loop(0, (count + 2 * GROUP - 1) // (2 * GROUP), two_groups, 0)
    note_load.wait()
    total = jnp.sum(notes[...].astype(jnp.float32), axis=0)
    half = D // 2
    gram[...] = total[:PACK, :half] + total[:PACK, half:] + total[PACK:, :half]
    for z in range(2 * GROUP):
        newest = z + 2 * GROUP * ((count - 1 - z) // (2 * GROUP))

        @pl.when((count > z) & (newest // GROUP * GROUP + 2 * GROUP >= count))
        def _(n=newest, z=z):
            save(n, z).wait()


def far_build(wanted, units, far_rows, rounded, after):
    peer_count = far_rows.shape[0]
    return pl.pallas_call(
        far_build_kernel,
        in_specs=[SMEM, HBM, HBM, VMEM, SMEM],
        out_specs=[VMEM, VMEM, HBM],
        out_shape=[
            jax.ShapeDtypeStruct((peer_count, VECS, BLK), jnp.bfloat16),
            jax.ShapeDtypeStruct((PACK, VECS * VECS // PACK), jnp.float32),
            pltpu.HBM((peer_count, BLK, BLK), jnp.bfloat16),
        ],
        scratch_shapes=[
            pltpu.SMEM((peer_count,), jnp.int32),
            pltpu.VMEM((peer_count, BLK, D), jnp.bfloat16),
            pltpu.VMEM((peer_count, BLK, D), jnp.bfloat16),
            pltpu.VMEM((2 * GROUP, BLK, BLK), jnp.bfloat16),
            pltpu.SemaphoreType.DMA((2, peer_count)),
            pltpu.SemaphoreType.DMA((2 * GROUP,)),
            pltpu.VMEM((peer_count, NOTE_ROWS, D), jnp.bfloat16),
            pltpu.SemaphoreType.DMA,
        ],
        compiler_params=params(28),
        cost_estimate=cost(32 * 2 * BLK * BLK * (D + 4 * VECS), 34 * 2**20),
        name="far_build",
    )(wanted, in_hbm(units), in_hbm(far_rows), rounded, after)


def stream(count, source_of, buffer, sem, base=0):
    def load(n):
        return pltpu.make_async_copy(source_of(n), buffer.at[base + n], sem.at[base + n])

    def begin(n, _):
        load(n).start()
        return 0

    lax.fori_loop(0, count, begin, 0)

    def work(use):
        def group(g, _):
            first = g * GROUP
            for z in range(GROUP):

                @pl.when(first + z < count)
                def _(n=first + z):
                    load(n).wait()

            held = [jnp.minimum(first + z, count - 1) for z in range(GROUP)]
            live = [first + z < count for z in range(GROUP)]
            use(held, live, [buffer.at[base + n] for n in held])
            return 0

        lax.fori_loop(0, (count + GROUP - 1) // GROUP, group, 0)

    return work


def tile_scratch(tiles):
    return [
        pltpu.VMEM((tiles, BLK, BLK), jnp.bfloat16),
        pltpu.SemaphoreType.DMA((tiles,)),
    ]


def masked(live, vecs):
    return jnp.where(live, vecs, jnp.zeros_like(vecs))


def own_apply_kernel(tiles, rounded, out, done, total, buffer, sem, save_sem):
    count = rounded.shape[1] // BLK - LATE
    done[0] = count
    total[:, count * BLK :] = jnp.zeros((VECS, LATE * BLK), jnp.float32)
    work = stream(count, lambda n: tiles.at[n], buffer, sem)

    def use(held, live, group):
        terms = [dot_nn(rounded[:, columns_of(n)], tile[...]) for n, tile in zip(held, group)]
        for n, term in zip(held, terms):
            total[:, columns_of(n)] = term

    work(use)
    save = pltpu.make_async_copy(total, out, save_sem)
    save.start()
    save.wait()


def own_apply(tiles, rounded):
    return pl.pallas_call(
        own_apply_kernel,
        in_specs=[HBM, VMEM],
        out_specs=[HBM, SMEM],
        out_shape=[
            pltpu.HBM(rounded.shape, jnp.float32),
            jax.ShapeDtypeStruct((1,), jnp.int32),
        ],
        scratch_shapes=[
            pltpu.VMEM(rounded.shape, jnp.float32),
            *tile_scratch(rounded.shape[1] // BLK),
            pltpu.SemaphoreType.DMA,
        ],
        compiler_params=params(20),
        cost_estimate=cost(24 * 2 * BLK * BLK * 4 * VECS, 13 * 2**20),
        name="own_apply",
    )(in_hbm(tiles), rounded)


def far_back_kernel(wanted, tiles, rounded, after, back, active, buffer, sem):
    del after
    count = note_active(wanted, active)
    work = stream(count, lambda n: tiles.at[active[n]], buffer, sem)

    def use(held, live, group):
        peers = [active[n] for n in held]
        terms = [
            dot_nn(rounded[:, columns_of(wanted[peer])], tile[...]) for peer, tile in zip(peers, group)
        ]
        for peer, term in zip(peers, terms):
            back[peer] = term.astype(jnp.bfloat16)

    work(use)


def far_back(wanted, tiles, rounded, after):
    peer_count = tiles.shape[0]
    return pl.pallas_call(
        far_back_kernel,
        in_specs=[SMEM, HBM, VMEM, SMEM],
        out_specs=VMEM,
        out_shape=jax.ShapeDtypeStruct((peer_count, VECS, BLK), jnp.bfloat16),
        scratch_shapes=[pltpu.SMEM((peer_count,), jnp.int32), *tile_scratch(peer_count)],
        compiler_params=params(24),
        cost_estimate=cost(32 * 2 * BLK * BLK * 4 * VECS, 17 * 2**20),
        name="far_back",
    )(wanted, in_hbm(tiles), rounded, after)


def add_far(wanted, far_vecs, total, active, work):
    def use(held, live, group):
        peers = [active[n] for n in held]
        terms = [
            dot_nt(masked(alive, far_vecs[peer]), tile[...])
            for peer, alive, tile in zip(peers, live, group)
        ]
        for peer, term in zip(peers, terms):
            total[:, columns_of(wanted[peer])] += term

    work(use)


def far_first_kernel(wanted, tiles, far_vecs, before, total, active, buffer, sem, before_sem):
    before_load = pltpu.make_async_copy(before, total, before_sem)
    before_load.start()
    count = note_active(wanted, active)
    work = stream(count, lambda n: tiles.at[active[n]], buffer, sem)
    before_load.wait()
    add_far(wanted, far_vecs, total, active, work)


def far_first(wanted, tiles, far_vecs, before):
    return pl.pallas_call(
        far_first_kernel,
        in_specs=[SMEM, HBM, VMEM, HBM],
        out_specs=VMEM,
        out_shape=jax.ShapeDtypeStruct(before.shape, jnp.float32),
        scratch_shapes=[
            pltpu.SMEM(wanted.shape, jnp.int32),
            *tile_scratch(wanted.shape[0]),
            pltpu.SemaphoreType.DMA,
        ],
        compiler_params=params(28),
        cost_estimate=cost(32 * 2 * BLK * BLK * 4 * VECS, 20 * 2**20),
        name="far_first",
    )(wanted, in_hbm(tiles), far_vecs, in_hbm(before))


def rest_apply_kernel(
    table, wanted, local_tiles, far_tiles, rounded, far_vecs, before, total, active, buffer, sem, before_sem
):
    block_count = rounded.shape[1] // BLK
    before_load = pltpu.make_async_copy(before, total, before_sem)
    before_load.start()
    crossed_work = stream(table[LOCAL_COUNT], lambda n: local_tiles.at[block_count + n], buffer, sem)
    early = block_count - LATE
    late_work = stream(LATE, lambda n: local_tiles.at[early + n], buffer, sem, EXTRA + wanted.shape[0])
    count = note_active(wanted, active)
    far_work = stream(count, lambda n: far_tiles.at[active[n]], buffer, sem, EXTRA)
    before_load.wait()

    def use_crossed(held, live, group):
        codes = [table[LOCAL + n] for n in held]
        pairs = [(code // 64, code % 64) for code in codes]
        vecs = [[masked(alive, rounded[:, columns_of(b)]) for b in pair] for pair, alive in zip(pairs, live)]
        to_col = [dot_nn(row_vecs, tile[...]) for (row_vecs, _), tile in zip(vecs, group)]
        to_row = [dot_nt(col_vecs, tile[...]) for (_, col_vecs), tile in zip(vecs, group)]
        for (row, col), row_term, col_term in zip(pairs, to_row, to_col):
            total[:, columns_of(col)] += col_term
            total[:, columns_of(row)] += row_term

    def use_late(held, live, group):
        terms = [dot_nn(rounded[:, columns_of(early + n)], tile[...]) for n, tile in zip(held, group)]
        for n, term in zip(held, terms):
            total[:, columns_of(early + n)] += term

    late_work(use_late)
    crossed_work(use_crossed)
    add_far(wanted, far_vecs, total, active, far_work)


def rest_apply(table, wanted, local_tiles, far_tiles, rounded, far_vecs, before):
    return pl.pallas_call(
        rest_apply_kernel,
        in_specs=[SMEM, SMEM, HBM, HBM, VMEM, VMEM, HBM],
        out_specs=VMEM,
        out_shape=jax.ShapeDtypeStruct(before.shape, jnp.float32),
        scratch_shapes=[
            pltpu.SMEM(wanted.shape, jnp.int32),
            *tile_scratch(EXTRA + wanted.shape[0] + LATE),
            pltpu.SemaphoreType.DMA,
        ],
        compiler_params=params(36),
        cost_estimate=cost(40 * 2 * BLK * BLK * 4 * VECS, 24 * 2**20),
        name="rest_apply",
    )(table, wanted, in_hbm(local_tiles), in_hbm(far_tiles), rounded, far_vecs, in_hbm(before))


def add_returned(table, own, returned, image):
    image[...] = own[...]

    def add(peer, _):
        row = table[FAR_ROW + peer]

        @pl.when(row >= 0)
        def _():
            image[:, columns_of(row)] += returned[peer].astype(jnp.float32)

        return 0

    lax.fori_loop(0, returned.shape[0], add, 0)


def gram_kernel(image, gram):
    total = jnp.zeros((3 * VECS, 3 * VECS), jnp.float32)
    for c in range(0, image.shape[1], CHUNK):
        total += products(image[:, c : c + CHUNK])
    gram[...] = packed(sum_of_parts(total))


def forward_kernel(table, own, returned, inverse, rounded, gram, send, image, sem):
    factor = factor_parts(inverse[...])
    add_returned(table, own, returned, image)

    def copy(peer, row):
        return pltpu.make_async_copy(rounded.at[:, columns_of(row)], send.at[peer], sem.at[peer])

    for c in range(0, image.shape[1], CHUNK):
        based = solved(factor, image[:, c : c + CHUNK])
        image[:, c : c + CHUNK] = based
        rounded[:, c : c + CHUNK] = based.astype(jnp.bfloat16)
        for block in range(c // BLK, (c + CHUNK) // BLK):
            each_peer_of(table, block, lambda peer, block=block: copy(peer, block).start())
    gram_kernel(image, gram)

    def finish(peer, _):
        row = table[FAR_ROW + peer]

        @pl.when(row >= 0)
        def _():
            copy(peer, row).wait()

        return 0

    lax.fori_loop(0, send.shape[0], finish, 0)


def forward(table, own, returned, inverse):
    return pl.pallas_call(
        forward_kernel,
        in_specs=[SMEM, VMEM, VMEM, VMEM],
        out_specs=[VMEM, VMEM, HBM],
        out_shape=[
            jax.ShapeDtypeStruct(own.shape, jnp.bfloat16),
            jax.ShapeDtypeStruct((PACK, VECS * VECS // PACK), jnp.float32),
            pltpu.HBM(returned.shape, jnp.bfloat16),
        ],
        scratch_shapes=[
            pltpu.VMEM(own.shape, jnp.float32),
            pltpu.SemaphoreType.DMA((returned.shape[0],)),
        ],
        compiler_params=params(12),
        cost_estimate=cost(10**8, 5 * 2**20),
        name="forward",
    )(table, own, returned, inverse)


def assemble_kernel(table, own, returned, image, gram):
    add_returned(table, own, returned, image)
    gram_kernel(image, gram)


def assemble(table, own, returned):
    return pl.pallas_call(
        assemble_kernel,
        in_specs=[SMEM, VMEM, VMEM],
        out_specs=[VMEM, VMEM],
        out_shape=[
            jax.ShapeDtypeStruct(own.shape, jnp.float32),
            jax.ShapeDtypeStruct((PACK, VECS * VECS // PACK), jnp.float32),
        ],
        compiler_params=params(10),
        cost_estimate=cost(10**8, 5 * 2**20),
        name="assemble",
    )(table, own, returned)


def inverse_factor(matrix):
    both = (VECS, 2 * VECS)
    rows = lax.broadcasted_iota(jnp.int32, both, 0)
    lanes = lax.broadcasted_iota(jnp.int32, both, 1)
    work = jnp.where(
        lanes < VECS,
        jnp.concatenate([matrix, matrix], axis=1),
        jnp.where(rows + VECS == lanes, 1.0, 0.0),
    )
    for k in range(0, VECS, 2):
        first_col = jnp.broadcast_to(work[:, k : k + 1], both)
        next_col = jnp.broadcast_to(work[:, k + 1 : k + 2], both)
        scale = lax.rsqrt(first_col[k : k + 1])
        first_row = work[k : k + 1] * scale
        cross = next_col[k : k + 1] * scale
        next_scale = lax.rsqrt(next_col[k + 1 : k + 2] - cross * cross)
        next_row = (work[k + 1 : k + 2] - cross * first_row) * next_scale
        first_factor = first_col * scale
        next_factor = (next_col - first_factor * cross) * next_scale
        rest = work - (first_factor * first_row + next_factor * next_row)
        kept = jnp.where(rows == k, first_row, jnp.where(rows == k + 1, next_row, work))
        work = jnp.where(rows > k + 1, rest, kept)
    return work[:, VECS:]


def identity():
    rows = lax.broadcasted_iota(jnp.int32, (VECS, VECS), 0)
    lanes = lax.broadcasted_iota(jnp.int32, (VECS, VECS), 1)
    return jnp.where(rows == lanes, 1.0, 0.0).astype(jnp.float32)


def basis_kernel(rows_all, gram, inverse):
    eye = identity()
    matrix = unpacked(gram[...]) * (1.0 / rows_all)
    factor = inverse_factor(matrix * (1.0 + 1e-3 * eye))
    usable = jnp.sum(jnp.abs(factor)) < 1e30
    inverse[...] = jnp.where(usable, factor, eye)


def basis(rows_all, gram):
    return pl.pallas_call(
        functools.partial(basis_kernel, rows_all),
        in_specs=[VMEM],
        out_specs=VMEM,
        out_shape=jax.ShapeDtypeStruct((VECS, VECS), jnp.float32),
        compiler_params=params(4),
        cost_estimate=cost(10**6, 10**4),
        name="basis",
    )(gram)


def last_kernel(rows_all, grams, image, out, vectors, sem):
    both = jnp.sum(grams[...], axis=0) * (1.0 / rows_all)
    first = inverse_factor(unpacked(both[:PACK]))
    high, middle, low = three_parts(first)
    turned = dot_nt(
        factor_parts(product(first, unpacked(both[PACK:]))),
        jnp.concatenate([high, middle, low, high, middle, high], axis=1),
    )
    factor = factor_parts(product(inverse_factor(turned), first))
    copies = []
    for c in range(0, image.shape[1], CHUNK):
        columns = pl.ds(c, CHUNK)
        vectors[:, columns] = solved(factor, image[:, columns])
        copies.append(pltpu.make_async_copy(vectors.at[:, columns], out.at[:, columns], sem.at[c // CHUNK]))
        copies[-1].start()
    for copy in copies:
        copy.wait()


def last(rows_all, grams, image):
    return pl.pallas_call(
        functools.partial(last_kernel, rows_all),
        in_specs=[VMEM, VMEM],
        out_specs=HBM,
        out_shape=jax.ShapeDtypeStruct(image.shape, jnp.float32),
        scratch_shapes=[
            pltpu.VMEM(image.shape, jnp.float32),
            pltpu.SemaphoreType.DMA((image.shape[1] // CHUNK,)),
        ],
        compiler_params=params(10),
        cost_estimate=cost(10**8, 4 * 2**20),
        name="last",
    )(grams, image)


def sum_over_gx(gram):
    size = lax.axis_size("gx")
    arrived = [
        lax.ppermute(gram, "gx", [(i, i ^ mask) for i in range(size)]) for mask in range(1, size)
    ]
    return sum(arrived, gram)


def all_parts(gram):
    gram = sum_over_gx(gram)
    return exchange(jnp.broadcast_to(gram, (lax.axis_size("gy"), *gram.shape)))


def exchange(blocks):
    return lax.all_to_all(blocks, "gy", split_axis=0, concat_axis=0, tiled=True)


def per_device(embeddings, start, requests, pairs, counts):
    rows_all = embeddings.shape[0] * lax.axis_size("gx") * lax.axis_size("gy")
    send_rows, rounded, table = prepare(embeddings, start, requests, pairs[0].T, counts)
    far_rows = exchange(send_rows)
    units, own, local_tiles, send_vecs, done = local_build(table, embeddings, rounded, requests.shape[1])
    far_vecs = exchange(send_vecs)
    wanted = far_rows[:, NOTE_BLOCK[0], NOTE_BLOCK[1]].astype(jnp.int32)
    back, start_gram, far_tiles = far_build(wanted, units, far_rows, rounded, done)
    returned = exchange(back)
    inverse = basis(rows_all, sum_over_gx(start_gram))
    own = far_first(wanted, far_tiles, far_vecs, own)
    rounded, first_gram, send_vecs = forward(table, own, returned, inverse)
    far_vecs = exchange(send_vecs)
    own, done = own_apply(local_tiles, rounded)
    returned = exchange(far_back(wanted, far_tiles, rounded, done))
    own = rest_apply(table, wanted, local_tiles, far_tiles, rounded, far_vecs, own)
    image, next_gram = assemble(table, own, returned)
    grams = all_parts(jnp.concatenate([first_gram, next_gram], axis=0))
    return last(rows_all, grams, image)


def solution(mesh):
    return jax.shard_map(
        per_device,
        mesh=mesh,
        in_specs=(
            P(("gx", "gy"), None),
            P(None, ("gx", "gy")),
            P(("gx", "gy"), None),
            P(("gx", "gy"), None, None),
            P(("gx", "gy")),
        ),
        out_specs=P(None, ("gx", "gy")),
        check_vma=False,
    )
```
